32 devices in a mesh: dp: 2 (over y), space: 16 (over z, x, core).
Axes of the slice: x: 2, y: 2, z: 4, core: 2. Of those that a mesh axis runs over, the one named last changes fastest.
Arguments:
- inputs: bfloat16 [28, 32, 32, 640], P('dp', 'space'), may hold values from -27 to 27
- norm_gain: float32 [640], replicated, may hold values from 0.1 to 1.9
- norm_bias: float32 [640], replicated, may hold values from -3 to 3
- conv_weight: bfloat16 [9, 640, 640], P(None, 'dp'), may hold values from -0.078125 to 0.078125
- upstream: bfloat16 [28, 32, 32, 640], P('dp', 'space'), may hold values from -6 to 6
Outputs:
- mixed: bfloat16 [28, 32, 32, 640], P('dp', 'space')
- input_grad: bfloat16 [28, 32, 32, 640], P('dp', 'space')
- weight_grad: float32 [9, 640, 640], P(None, 'dp', 'space')
- gain_grad: float32 [640], replicated
- bias_grad: float32 [640], replicated
The draws below stay inside these ranges and needn't reach their ends.
All inputs are finite; a program needn't handle non-finite values.
Results may differ from the reference program's by a relative error of at most 0.0031.
Values may be sent and summed in bfloat16 or wider, within the bound.
No kernel may reach another device: no remote copies, remote signals or barrier semaphores. Data moves between devices by JAX's collectives and lax.ppermute only.
A program may use at most 128 MiB of HBM per device.

```python
import jax
import jax.numpy as jnp
from jax import lax

C = 640
GSIZE = 40
WIDTH = 32
HEIGHT = 32
IMAGES = 28


def draw_inputs(key, part):
    noise_key, scale_key = jax.random.split(key, 2)
    heights = jnp.arange(HEIGHT, dtype=jnp.float32) / max(HEIGHT - 1, 1)
    rising = 0.5 * jnp.exp(heights * jnp.log(3.0))
    channel_scale = jnp.exp(jax.random.uniform(scale_key, (IMAGES, 1, 1, C), jnp.float32, jnp.log(0.3), jnp.log(3.0)))
    values = jnp.clip(jax.random.normal(noise_key, (IMAGES, HEIGHT, WIDTH, C), jnp.float32), -6.0, 6.0)
    return (values * rising[None, :, None, None] * channel_scale).astype(jnp.bfloat16)


def with_spikes(entries, key, source, target, shards_of, factor):
    def block_of(axis_at):
        return (jnp.arange(entries.shape[axis_at]) // (entries.shape[axis_at] // shards_of)).reshape((-1,) + (1,) * (entries.ndim - 1 - axis_at))

    first = jax.random.permutation(key, shards_of)[block_of(target)]
    second = (block_of(target) + shards_of // 2) % shards_of
    return jnp.where((block_of(source) == first) | (block_of(source) == second), factor * entries, entries)


def level_of(own_key, dims, cuts, least, largest):
    factor_of, own = 1.0, jax.random.fold_in(own_key, 6)
    for position, shards_of in cuts:
        steps = jnp.exp(jax.random.uniform(jax.random.fold_in(own, position), (shards_of,), jnp.float32, least / len(cuts), largest / len(cuts)))
        factor_of = factor_of * jnp.repeat(steps, dims[position] // shards_of).reshape([-1 if axis == position else 1 for axis in range(len(dims))])
    return factor_of


def noise(stream_key, dims, deviation, most, shards=(), held_as=jnp.bfloat16):
    values = deviation * jax.random.normal(stream_key, dims, jnp.float32)
    if shards:
        values = values * level_of(stream_key, dims, shards, -0.22, 0.18)
    return jnp.clip(values, -most, most).astype(held_as)


def noise_with(stream_key, dims, width, bound, cuts, heavy, held_as=jnp.bfloat16):
    result = width * jax.random.normal(stream_key, dims, jnp.float32)
    if cuts:
        result = result * level_of(stream_key, dims, cuts, -0.22, 0.18)
    return jnp.clip(with_spikes(result, jax.random.fold_in(stream_key, 3), *heavy), -bound, bound).astype(held_as)


def setup_inputs(seed: int = 0) -> dict:
    key_of = jax.random.split(jax.random.key(seed), 6)
    return {
        "inputs": draw_inputs(jax.random.fold_in(key_of[5], 71), 0),
        "norm_gain": jnp.clip(1.0 + 0.18 * jax.random.normal(key_of[1], (C,), jnp.float32), 0.1, 1.9),
        "norm_bias": noise(key_of[2], (C,), 0.5, 3.0, (), jnp.float32),
        "conv_weight": noise(key_of[3], (9, C, C), (9 * C) ** -0.5, 0.078125, ((1, 2),)),
        "upstream": noise_with(key_of[4], (IMAGES, HEIGHT, WIDTH, C), 1.0, 6.0, ((0, 2), (1, 16)), (1, 3, 16, 2.0)),
    }


EPS = 1e-05

def group_means(values, count):
    image_count, height_all, width_all, channels = values.shape
    grouped = values.reshape(image_count, height_all, width_all, channels // GSIZE, GSIZE)
    return lax.optimization_barrier(jnp.sum(grouped, axis=(1, 2, 4))) / count

def spread_groups(group_vals):
    return jnp.repeat(group_vals, GSIZE, axis=1)[:, None, None, :]

def reference(inputs, norm_gain, norm_bias, conv_weight, upstream):
    x_float = inputs.astype(jnp.float32)
    image_count, height_all, width_all, channels = x_float.shape
    count = float(height_all * width_all * GSIZE)
    group_mean = group_means(x_float, count)
    group_square = group_means(x_float * x_float, count)
    group_rstd = lax.rsqrt(group_square - group_mean * group_mean + EPS)
    mean_chan = spread_groups(group_mean)
    rstd_chan = spread_groups(group_rstd)
    centred = (x_float - mean_chan) * rstd_chan
    normed = centred * norm_gain + norm_bias
    activated = jax.nn.silu(normed).astype(jnp.bfloat16)
    act_pad = jnp.pad(activated, ((0, 0), (1, 1), (1, 1), (0, 0)))
    grad_pad = jnp.pad(upstream, ((0, 0), (1, 1), (1, 1), (0, 0)))
    upstream_flat = upstream.reshape(-1, channels)
    conv_out = jnp.zeros((upstream_flat.shape[0], channels), jnp.float32)
    act_grad = jnp.zeros((upstream_flat.shape[0], channels), jnp.float32)
    grad_list = []
    for tap_row in range(3):
        for tap_col in range(3):
            tap_index = 3 * tap_row + tap_col
            act_window = act_pad[:, tap_row:tap_row + height_all, tap_col:tap_col + width_all, :].reshape(-1, channels)
            grad_window = grad_pad[:, 2 - tap_row:2 - tap_row + height_all, 2 - tap_col:2 - tap_col + width_all, :].reshape(-1, channels)
            conv_out = conv_out + jnp.dot(act_window, conv_weight[tap_index], preferred_element_type=jnp.float32)
            act_grad = act_grad + jnp.dot(grad_window, conv_weight[tap_index].T, preferred_element_type=jnp.float32)
            grad_list.append(jnp.dot(act_window.T, upstream_flat, preferred_element_type=jnp.float32))
    mixed = (x_float + conv_out.reshape(x_float.shape)).astype(jnp.bfloat16)
    weight_grad = jnp.stack(grad_list)
    sigmoid_n = jax.nn.sigmoid(normed)
    normed_grad = act_grad.reshape(x_float.shape) * sigmoid_n * (1.0 + normed * (1.0 - sigmoid_n))
    gain_grad = lax.optimization_barrier(jnp.sum(normed_grad * centred, axis=(0, 1, 2)))
    bias_grad = lax.optimization_barrier(jnp.sum(normed_grad, axis=(0, 1, 2)))
    centred_grad = normed_grad * norm_gain
    first_mean = spread_groups(group_means(centred_grad, count))
    second_mean = spread_groups(group_means(centred_grad * centred, count))
    input_grad = (upstream.astype(jnp.float32) + rstd_chan * (centred_grad - first_mean - centred * second_mean)).astype(jnp.bfloat16)
    return (mixed, input_grad, weight_grad, gain_grad, bias_grad)
```

```python
import functools

import jax
import jax.numpy as jnp
from jax import lax
from jax.experimental import pallas as pl
from jax.experimental.pallas import tpu as pltpu
from jax.sharding import PartitionSpec as P

GSIZE = 40
EPS = 1e-05
GROUP_A, GROUP_B = (0, 1, 2, 3, 4), (5, 6, 7, 8)
LANES = 128
F32 = jnp.float32
BF16 = jnp.bfloat16
HIGHEST = lax.Precision.HIGHEST
VMEM_SPEC = pl.BlockSpec(memory_space=pltpu.VMEM)
SMEM_SPEC = pl.BlockSpec(memory_space=pltpu.SMEM)
HBM_SPEC = pl.BlockSpec(memory_space=pltpu.HBM)
MIB = 1 << 20
V, S, H = VMEM_SPEC, SMEM_SPEC, HBM_SPEC


def kernel_call(body, mib, out_shape, in_specs, name, scratch=(), out_specs=None):
    return pl.pallas_call(
        body,
        out_shape=out_shape,
        in_specs=in_specs,
        out_specs=out_specs or jax.tree.map(lambda _: VMEM_SPEC, out_shape),
        scratch_shapes=scratch,
        compiler_params=pltpu.CompilerParams(vmem_limit_bytes=mib * MIB),
        name=name,
    )


def struct(shape, dtype):
    return jax.ShapeDtypeStruct(shape, dtype)


def swap(value, axis, bit):
    count = lax.axis_size(axis)
    return lax.ppermute(value, axis, [(i, i ^ bit) for i in range(count)])


def after(value, *others):
    return lax.optimization_barrier((value,) + others)[0]


def members(channels, groups):
    chan = lax.broadcasted_iota(jnp.int32, (groups, channels), 1)
    first = lax.broadcasted_iota(jnp.int32, (groups, channels), 0) * GSIZE
    return ((chan >= first) & (chan < first + GSIZE)).astype(F32)


def to_groups(sums, member):
    return lax.dot_general(
        sums, member, (((1,), (1,)), ((), ())), precision=HIGHEST, preferred_element_type=F32
    )


def to_chans(values, member):
    return jnp.dot(values, member, precision=HIGHEST, preferred_element_type=F32)


def shifted(block):
    columns = block.shape[0]
    col = lax.broadcasted_iota(jnp.int32, block.shape, 0)
    down = jnp.where(col == 0, 0.0, pltpu.roll(block, 1, axis=0))
    up = jnp.where(col == columns - 1, 0.0, pltpu.roll(block, columns - 1, axis=0))
    return down, up


def stats_kernel(info, x, u, *refs):
    if len(refs) == 7:
        w, out, edge_x, edge_u, w_first, w_last, sem = refs
    else:
        out, edge_x, edge_u, sem = refs
    images, _, _, channels = x.shape
    core = info[0]
    copies = [
        pltpu.make_async_copy(x.at[:, core], edge_x, sem.at[0]),
        pltpu.make_async_copy(u.at[:, core], edge_u, sem.at[1]),
    ]
    if len(refs) == 7:
        part, rows = w.shape[1] // 2, w_last.shape[1]
        for k, (start, dst) in enumerate(((info[4] * 3 * rows, w_first), (2 * rows, w_last))):
            at = pl.ds(pl.multiple_of(core * part + start, 32), dst.shape[1])
            copies.append(pltpu.make_async_copy(w.at[:, at, :], dst, sem.at[2 + k]))
    for c in copies:
        c.start()
    one, two = [], []
    for img in range(images):
        value = x[img].astype(F32).reshape(-1, channels)
        one.append(jnp.sum(value, axis=0, keepdims=True))
        two.append(jnp.sum(value * value, axis=0, keepdims=True))
    out[...] = to_groups(jnp.concatenate(one + two), members(channels, channels // GSIZE))
    for c in copies:
        c.wait()


def act_kernel(size, info, stats, x, x_mate, rim, rim_mate, gain, bias, mid, side, mean, rstd):
    images, _, columns, channels = x.shape
    core, own_ok, mate_ok = info[0], info[1], info[2]
    member = members(channels, channels // GSIZE)
    group_mean = stats[:images] / size
    group_rstd = lax.rsqrt(stats[images:] / size - group_mean * group_mean + EPS)
    mean[...] = to_chans(group_mean, member)
    rstd[...] = to_chans(group_rstd, member)

    def fill(load, row, keep):
        def step(img, carry):
            value = load(img).astype(F32)
            scale = rstd[pl.ds(img, 1), :] * gain[...]
            normed = (value - mean[pl.ds(img, 1), :]) * scale + bias[...]
            act = normed / (1.0 + jnp.exp(-normed))
            if keep is not None:
                act = jnp.where(keep > 0, act, 0.0)
            down, up = shifted(act)
            at = pl.ds(pl.multiple_of((row * images + img) * columns, columns), columns)
            mid[at, :] = act.astype(BF16)
            side[0, at, :] = down.astype(BF16)
            side[1, at, :] = up.astype(BF16)
            return carry

        lax.fori_loop(0, images, step, 0)

    fill(lambda img: x[img, 0], 1 + 2 * core, None)
    fill(lambda img: x[img, 1], 2 + 2 * core, None)
    fill(lambda img: x_mate[img, 0], 3 - 2 * core, None)
    fill(lambda img: x_mate[img, 1], 4 - 2 * core, None)
    fill(lambda img: rim[img], 5 * core, own_ok)
    fill(lambda img: rim_mate[img], 5 - 5 * core, mate_ok)


def turn_kernel(bits, info, u, u_mate, out, rows):
    images, _, columns, channels = u.shape
    core, me = info[0], info[5]
    block = images * columns
    for r in range(2):
        at = pl.multiple_of((r + 2 * core) * block, 64)
        rows[pl.ds(at, block), :] = u[:, r].reshape(block, channels)
        at = pl.multiple_of((r + 2 - 2 * core) * block, 64)
        rows[pl.ds(at, block), :] = u_mate[:, r].reshape(block, channels)
    width = channels >> bits
    row = lax.broadcasted_iota(jnp.int32, out.shape[:1] + (channels,), 0)
    chan = core * width + row
    for place in range(bits - 1):
        low = width << (bits - 2 - place)
        own = (me >> (place + 1)) & 1
        late = lax.rem(row, 2 * low) >= low
        chan = chan - jnp.where(late, low, 0)
        bit = jnp.where(late, own, 1 - own)
        chan = chan + bit * (width << (place + 1))
    index = lax.broadcasted_iota(jnp.int32, chan.shape, 1)
    table = (index == chan).astype(F32).astype(BF16)
    out[...] = lax.dot_general(
        table, rows[...], (((1,), (1,)), ((), ())), preferred_element_type=F32
    ).astype(BF16)


def tap_block(mid, side, t, start, rows):
    at = pl.ds(start, rows)
    return mid[at, :] if t % 3 == 1 else side[(t % 3) // 2, at, :]


def halves(value, part):
    taps = value.shape[1] // (2 * part)
    low = [value[:, 2 * t * part : (2 * t + 1) * part] for t in range(taps)]
    high = [value[:, (2 * t + 1) * part : (2 * t + 2) * part] for t in range(taps)]
    return jnp.concatenate(low, axis=1), jnp.concatenate(high, axis=1)


def grad_kernel(taps, block, by_dp, info, lhs, mid, side, sent, kept):
    channels = mid.shape[1]
    cut = lhs.shape[0] // 2
    for first in range(0, len(taps), 2):
        pair = taps[first : first + 2]
        rhs = [tap_block(mid, side, t, (t // 3) * block, lhs.shape[1]) for t in pair]
        rhs = rhs[0] if len(rhs) == 1 else jnp.concatenate(rhs, axis=1)
        got = jnp.dot(lhs[...], rhs, preferred_element_type=F32)
        if by_dp:
            low, high = halves(got, channels // 2)
            at = slice(first * channels // 2, first * channels // 2 + low.shape[1])
            sent[:, at] = jnp.where(info[3] == 0, high, low).astype(BF16)
            kept[:, at] = jnp.where(info[3] == 0, low, high)
        else:
            at = slice(first * channels, first * channels + rhs.shape[1])
            sent[:, at] = got[:cut].astype(BF16)
            kept[:, at] = got[cut:]


def fold_kernel(kept, got, sent_out, kept_out):
    cut = sent_out.shape[0]
    sent_out[...] = (kept[:cut] + got[:cut].astype(F32)).astype(BF16)
    kept_out[...] = kept[cut:] + got[cut:].astype(F32)


def part_kernel(part, info, kept, got, sent_out, kept_out):
    low, high = halves(kept[...] + got[...].astype(F32), part)
    sent_out[...] = jnp.where(info[3] == 0, high, low).astype(BF16)
    kept_out[...] = jnp.where(info[3] == 0, low, high)


def weights_kernel(places, *refs):
    parts, out = refs[:-1], refs[-1]
    for k, part in enumerate(parts):
        at = pl.ds(pl.multiple_of(places[k], 32), part.shape[1])
        for t in range(out.shape[0]):
            out[t, at, :] = part[t]


def conv_kernel(info, mid, w, x, out, side):
    images, _, columns, channels = x.shape
    block = images * columns
    first = pl.multiple_of(2 * info[0] * block, 64)
    taps = w.shape[0]

    def fill(k, carry):
        at = pl.multiple_of(k * columns, columns)
        down, up = shifted(mid[pl.ds(first + at, columns), :].astype(F32))
        side[0, pl.ds(at, columns), :] = down.astype(BF16)
        side[1, pl.ds(at, columns), :] = up.astype(BF16)
        return carry

    lax.fori_loop(0, 4 * images, fill, 0)
    rhs = w[...].reshape(taps * channels, channels)
    for r in range(2):
        lhs = []
        for t in range(taps):
            at = (r + t // 3) * block
            if t % 3 == 1:
                lhs.append(mid[pl.ds(pl.multiple_of(first + at, 64), block), :])
            else:
                lhs.append(side[(t % 3) // 2, at : at + block, :])
        lhs = jnp.concatenate(lhs, axis=1)
        value = jnp.dot(lhs, rhs, preferred_element_type=F32).reshape(images, columns, channels)
        out[:, r] = (x[:, r].astype(F32) + value).astype(BF16)


def back_kernel(info, u, u_mate, rim, w, x, mean, rstd, gain, bias, out, sums, part, one, two):
    images, _, columns, channels = x.shape
    block = images * columns
    taps = w.shape[0]
    core = info[0]

    def fill(load, row):
        def step(img, carry):
            value = load(img)
            down, up = shifted(value.astype(F32))
            at = pl.ds(pl.multiple_of((row * images + img) * columns, columns), columns)
            part[0, at, :] = down.astype(BF16)
            part[1, at, :] = value
            part[2, at, :] = up.astype(BF16)
            return carry

        lax.fori_loop(0, images, step, 0)

    fill(lambda img: u[img, 0], 1)
    fill(lambda img: u[img, 1], 2)
    fill(lambda img: u_mate[img, core], 3 - 3 * core)
    fill(lambda img: rim[img], 3 * core)

    rhs = jnp.concatenate([w[t] for t in range(taps)], axis=1)
    for r in range(2):
        lhs = jnp.concatenate([
            part[2 - t % 3, (r + 2 - t // 3) * block : (r + 3 - t // 3) * block, :]
            for t in range(taps)
        ], axis=1)
        out[:, r] = lax.dot_general(
            lhs, rhs, (((1,), (1,)), ((), ())), preferred_element_type=F32
        ).reshape(images, columns, channels)

    def finish(img, carry):
        first = jnp.zeros((1, channels), F32)
        second = jnp.zeros((1, channels), F32)
        for r in range(2):
            centred = (x[img, r].astype(F32) - mean[pl.ds(img, 1), :]) * rstd[pl.ds(img, 1), :]
            normed = centred * gain[...] + bias[...]
            s = 1.0 / (1.0 + jnp.exp(-normed))
            grad = out[img, r] * s * (1.0 + normed * (1.0 - s))
            out[img, r] = grad
            first = first + jnp.sum(grad, axis=0, keepdims=True)
            second = second + jnp.sum(grad * centred, axis=0, keepdims=True)
        one[pl.ds(img, 1), :] = first
        two[pl.ds(img, 1), :] = second
        return carry

    lax.fori_loop(0, images, finish, 0)
    groups = channels // GSIZE
    member = members(channels, groups)
    sums[...] = jnp.zeros_like(sums)
    sums[0:images, 0:groups] = to_groups(one[...] * gain[...], member)
    sums[0:images, groups : 2 * groups] = to_groups(two[...] * gain[...], member)
    base = images + images % 2
    rows = channels // LANES
    gain_part = jnp.sum(two[...], axis=0, keepdims=True)
    bias_part = jnp.sum(one[...], axis=0, keepdims=True)
    for k in range(rows):
        at = slice(k * LANES, (k + 1) * LANES)
        sums[base + k : base + k + 1, :] = gain_part[:, at]
        sums[base + rows + k : base + rows + k + 1, :] = bias_part[:, at]


def input_kernel(size, sums, grad, x, u, mean, rstd, gain, out):
    images, rows, columns, channels = x.shape
    groups = channels // GSIZE
    member = members(channels, groups)
    means = sums[...] / size
    first = to_chans(means[:images, :groups], member)
    second = to_chans(means[:images, groups : 2 * groups], member)
    for img in range(images):
        at = slice(img, img + 1)
        for r in range(rows):
            centred = (x[img, r].astype(F32) - mean[at]) * rstd[at]
            inner = grad[img, r] * gain[...] - first[at] - centred * second[at]
            out[img, r] = (u[img, r].astype(F32) + rstd[at] * inner).astype(BF16)


def body(inputs, norm_gain, norm_bias, conv_weight, upstream):
    images, rows, columns, channels = inputs.shape
    count, dps = lax.axis_size("space"), lax.axis_size("dp")
    me, half = lax.axis_index("space"), lax.axis_index("dp")
    core, mate, side_bit = me & 1, me ^ 1, (me >> 2) & 1
    groups = channels // GSIZE
    bits = count.bit_length() - 1
    size = float(rows * columns * GSIZE * count)
    block = images * columns
    two = dps == 2
    gain_row, bias_row = norm_gain[None], norm_bias[None]
    taps = conv_weight.shape[0]
    own_ok = jnp.where((me == 0) | (me == count - 1), 0, 1)
    mate_ok = jnp.where((mate == 0) | (mate == count - 1), 0, 1)
    info = jnp.stack(
        [core, own_ok, mate_ok, half if two else 0 * core, side_bit, me]
    ).astype(jnp.int32)

    pairs = []
    for i in range(1, count - 1, 2):
        pairs += [(i, i + 1), (i + 1, i)]
    x_mate = swap(inputs, "space", 1)
    u_mate = swap(upstream, "space", 1)

    part = conv_weight.shape[1] // 2
    fifth = part // 5
    row_shape = (images, columns, channels)
    out_shape = [struct((2 * images, groups), F32), struct(row_shape, BF16), struct(row_shape, BF16)]
    operands = [info, inputs, upstream]
    if two:
        out_shape += [
            struct((taps, 2 * fifth, channels), BF16), struct((taps, fifth, channels), BF16)
        ]
        operands.append(conv_weight)
    stats, edge_x, edge_u, *w_sent = kernel_call(
        stats_kernel, 16, tuple(out_shape), [S, V, H] + [H] * (len(operands) - 3), "stats",
        [pltpu.SemaphoreType.DMA((4,))], (V,) + (H,) * (len(out_shape) - 1),
    )(*operands)
    rim_x = lax.ppermute(edge_x, "space", pairs)
    for place in [0] + list(range(2, bits)) + [1]:
        if place == 1:
            stats, rim_x = lax.optimization_barrier((stats, rim_x))
        stats = stats + swap(stats, "space", 1 << place)
        if two and place == 2:
            w_first = swap(after(w_sent[0], stats), "dp", 1)
        if two and place == 3:
            w_last = swap(after(w_sent[1], stats), "dp", 1)
    rim_x_mate = swap(rim_x, "space", 1)
    rim_u = lax.ppermute(after(edge_u, stats), "space", pairs)
    if two:
        w_second = swap(after(w_first, stats), "space", 4)

    act_mid, act_side, mean, rstd = kernel_call(
        functools.partial(act_kernel, size), 24,
        (
            struct((6 * block, channels), BF16),
            struct((2, 6 * block, channels), BF16),
            struct((images, channels), F32),
            struct((images, channels), F32),
        ),
        [S] + [V] * 7, "activate",
    )(info, stats, inputs, x_mate, rim_x, rim_x_mate, gain_row, bias_row)

    lhs = kernel_call(
        functools.partial(turn_kernel, bits), 16, struct((channels // 2, 4 * block), BF16),
        [S, V, V], "turn", [pltpu.VMEM((4 * block, channels), BF16)],
    )(info, upstream, u_mate)

    def terms(group, by_dp, lhs):
        width = len(group) * channels
        shape = (channels // 2, width // 2) if by_dp else (channels // 4, width)
        return kernel_call(
            functools.partial(grad_kernel, group, block, by_dp), 28,
            (struct(shape, BF16), struct(shape, F32)), [S] + [V] * 3, "weight_terms",
        )(info, lhs, act_mid, act_side)

    def fold(kept, got):
        shape = (kept.shape[0] // 2, kept.shape[1])
        return kernel_call(
            fold_kernel, 8, (struct(shape, BF16), struct(shape, F32)), [V, V], "fold"
        )(kept, got)

    def split(kept, got):
        shape = (kept.shape[0], kept.shape[1] // 2)
        return kernel_call(
            functools.partial(part_kernel, channels // 2), 8,
            (struct(shape, BF16), struct(shape, F32)), [S, V, V], "split",
        )(info, kept, got)

    sent_a, kept_a = terms(GROUP_A, False, lhs)
    got_a = swap(sent_a, "space", 2)
    sent_b, kept_b = terms(GROUP_B, two, after(lhs, sent_a, rim_u))
    got_b = swap(sent_b, "dp", 1) if two else swap(sent_b, "space", 2)

    if two:
        w_parts = list(lax.optimization_barrier((w_first, w_second, w_last, sent_a))[:3])
        w_parts += [swap(value, "space", 1) for value in w_parts]
        other = (1 - half) * 2 * part
        spots = [half * 2 * part]
        for which in (core, 1 - core):
            spots += [
                other + which * part + side_bit * 3 * fifth,
                other + which * part + (1 - side_bit) * 3 * fifth,
                other + which * part + 2 * fifth,
            ]
        weights = kernel_call(
            weights_kernel, 20, struct((taps, channels, channels), BF16), [S] + [V] * 7, "weights",
        )(jnp.stack(spots).astype(jnp.int32), after(conv_weight, sent_b), *w_parts)
    else:
        weights = lax.all_gather(conv_weight, "dp", axis=1, tiled=True)

    grad, sums = kernel_call(
        back_kernel, 32,
        (struct(inputs.shape, F32), struct((40, LANES), F32)), [S] + [V] * 9, "conv_backward",
        [
            pltpu.VMEM((3, 4 * block, channels), BF16),
            pltpu.VMEM((images, channels), F32),
            pltpu.VMEM((images, channels), F32),
        ],
    )(info, upstream, u_mate, rim_u, weights, inputs, mean, rstd, gain_row, bias_row)

    sums = sums + swap(sums, "space", 1)
    step = swap(sums, "space", 4)
    if two:
        sent_b, kept_b = fold(kept_b, after(got_b, sums))
        got_b = swap(sent_b, "space", 2)
    else:
        sent_b, kept_b = fold(kept_b, after(got_b, sums))
        got_b = swap(sent_b, "space", 4)
    sent_a, kept_a = fold(kept_a, after(got_a, sent_b))
    got_a = swap(sent_a, "space", 4)

    mixed = kernel_call(
        conv_kernel, 28, struct(inputs.shape, BF16), [S] + [V] * 3, "conv_forward",
        [pltpu.VMEM((2, 4 * block, channels), BF16)],
    )(after(info, sent_a, sent_b), act_mid, weights, inputs)

    sums = sums + after(step, mixed)
    step = swap(sums, "space", 8)
    if two:
        sent_a, kept_a = split(kept_a, after(got_a, mixed))
        got_a = swap(sent_a, "dp", 1)
        sent_b, kept_b = fold(kept_b, after(got_b, sent_a))
        got_b = swap(sent_b, "space", 4)
    sums = sums + after(step, sent_b)
    sums = sums + swap(sums, "space", 2)
    input_grad = kernel_call(
        functools.partial(input_kernel, size), 16, struct(inputs.shape, BF16), [V] * 7, "input_grad"
    )(sums, grad, inputs, upstream, mean, rstd, gain_row)

    base = images + images % 2
    totals = sums[base : base + 2 * channels // LANES]
    totals = totals + swap(totals, "dp", 1) if two else lax.psum(totals, "dp")
    totals = totals.reshape(2, channels)

    sent_a, kept_a = fold(kept_a, after(got_a, input_grad))
    got_a = swap(sent_a, "space", 8)
    sent_b, kept_b = fold(kept_b, after(got_b, sent_a))
    got_b = swap(sent_b, "space", 8)
    weight_grad = jnp.concatenate(
        [kept_a + got_a.astype(F32), kept_b + got_b.astype(F32)], axis=1
    )
    weight_grad = weight_grad.reshape(weight_grad.shape[0], taps, -1)
    if not two:
        weight_grad = lax.psum_scatter(weight_grad, "dp", scatter_dimension=2, tiled=True)
    weight_grad = weight_grad.transpose(1, 2, 0)
    return (mixed, input_grad, weight_grad, totals[0], totals[1])


def solution(mesh):
    in_specs = (
        P("dp", "space", None, None),
        P(),
        P(),
        P(None, "dp", None),
        P("dp", "space", None, None),
    )
    out_specs = (
        P("dp", "space", None, None),
        P("dp", "space", None, None),
        P(None, "dp", "space"),
        P(),
        P(),
    )
    return jax.shard_map(body, mesh=mesh, in_specs=in_specs, out_specs=out_specs, check_vma=False)
```

```python
import functools

import jax
import jax.numpy as jnp
from jax import lax
from jax.experimental import pallas as pl
from jax.experimental.pallas import tpu as pltpu
from jax.sharding import PartitionSpec as P

GSIZE = 40
EPS = 1e-05
GROUP_A, GROUP_B = (0, 1, 2, 3), (4, 5, 6, 7, 8)
LANES = 128
F32 = jnp.float32
BF16 = jnp.bfloat16
HIGHEST = lax.Precision.HIGHEST
VMEM_SPEC = pl.BlockSpec(memory_space=pltpu.VMEM)
SMEM_SPEC = pl.BlockSpec(memory_space=pltpu.SMEM)
HBM_SPEC = pl.BlockSpec(memory_space=pltpu.HBM)
MIB = 1 << 20
V, S, H = VMEM_SPEC, SMEM_SPEC, HBM_SPEC


def kernel_call(body, mib, out_shape, in_specs, name, scratch=(), out_specs=None):
    return pl.pallas_call(
        body,
        out_shape=out_shape,
        in_specs=in_specs,
        out_specs=out_specs or jax.tree.map(lambda _: VMEM_SPEC, out_shape),
        scratch_shapes=scratch,
        compiler_params=pltpu.CompilerParams(vmem_limit_bytes=mib * MIB),
        name=name,
    )


def struct(shape, dtype):
    return jax.ShapeDtypeStruct(shape, dtype)


def swap(value, axis, bit):
    count = lax.axis_size(axis)
    return lax.ppermute(value, axis, [(i, i ^ bit) for i in range(count)])


def in_hbm(value):
    return pltpu.with_memory_space_constraint(value, pltpu.HBM)


def after(value, *others):
    return lax.optimization_barrier((value,) + others)[0]


def members(channels, groups):
    chan = lax.broadcasted_iota(jnp.int32, (groups, channels), 1)
    first = lax.broadcasted_iota(jnp.int32, (groups, channels), 0) * GSIZE
    return ((chan >= first) & (chan < first + GSIZE)).astype(F32)


def to_groups(sums, member):
    return lax.dot_general(
        sums, member, (((1,), (1,)), ((), ())), precision=HIGHEST, preferred_element_type=F32
    )


def to_chans(values, member):
    return jnp.dot(values, member, precision=HIGHEST, preferred_element_type=F32)


def shifted(block):
    columns = block.shape[0]
    col = lax.broadcasted_iota(jnp.int32, block.shape, 0)
    down = jnp.where(col == 0, 0.0, pltpu.roll(block, 1, axis=0))
    up = jnp.where(col == columns - 1, 0.0, pltpu.roll(block, columns - 1, axis=0))
    return down, up


def stats_kernel(info, x, u, *refs):
    if len(refs) == 6:
        w, out, edge_x, edge_u, w_sent, sem = refs
    else:
        out, edge_x, edge_u, sem = refs
    images, _, _, channels = x.shape
    core = info[0]
    copies = [
        pltpu.make_async_copy(x.at[:, core], edge_x, sem.at[0]),
        pltpu.make_async_copy(u.at[:, core], edge_u, sem.at[1]),
    ]
    if len(refs) == 6:
        rows = w_sent.shape[1]
        at = pl.ds(pl.multiple_of(core * rows, 32), rows)
        copies.append(pltpu.make_async_copy(w.at[:, at, :], w_sent, sem.at[2]))
    for c in copies:
        c.start()
    one, two = [], []
    for img in range(images):
        value = x[img].astype(F32).reshape(-1, channels)
        one.append(jnp.sum(value, axis=0, keepdims=True))
        two.append(jnp.sum(value * value, axis=0, keepdims=True))
    out[...] = to_groups(jnp.concatenate(one + two), members(channels, channels // GSIZE))
    for c in copies:
        c.wait()


def act_kernel(size, info, stats, x, x_mate, rim, rim_mate, gain, bias, mid, side, mean, rstd):
    images, _, columns, channels = x.shape
    core, own_ok, mate_ok = info[0], info[1], info[2]
    member = members(channels, channels // GSIZE)
    group_mean = stats[:images] / size
    group_rstd = lax.rsqrt(stats[images:] / size - group_mean * group_mean + EPS)
    mean[...] = to_chans(group_mean, member)
    rstd[...] = to_chans(group_rstd, member)

    def fill(load, row, keep):
        def step(img, carry):
            value = load(img).astype(F32)
            scale = rstd[pl.ds(img, 1), :] * gain[...]
            normed = (value - mean[pl.ds(img, 1), :]) * scale + bias[...]
            act = normed / (1.0 + jnp.exp(-normed))
            if keep is not None:
                act = jnp.where(keep > 0, act, 0.0)
            down, up = shifted(act)
            at = pl.ds(pl.multiple_of((row * images + img) * columns, columns), columns)
            mid[at, :] = act.astype(BF16)
            side[0, at, :] = down.astype(BF16)
            side[1, at, :] = up.astype(BF16)
            return carry

        lax.fori_loop(0, images, step, 0)

    fill(lambda img: x[img, 0], 1 + 2 * core, None)
    fill(lambda img: x[img, 1], 2 + 2 * core, None)
    fill(lambda img: x_mate[img, 0], 3 - 2 * core, None)
    fill(lambda img: x_mate[img, 1], 4 - 2 * core, None)
    fill(lambda img: rim[img], 5 * core, own_ok)
    fill(lambda img: rim_mate[img], 5 - 5 * core, mate_ok)


def turn_kernel(bits, info, u, u_mate, out, rows):
    images, _, columns, channels = u.shape
    core, me = info[0], info[4]
    block = images * columns
    for r in range(2):
        at = pl.multiple_of((r + 2 * core) * block, 64)
        rows[pl.ds(at, block), :] = u[:, r].reshape(block, channels)
        at = pl.multiple_of((r + 2 - 2 * core) * block, 64)
        rows[pl.ds(at, block), :] = u_mate[:, r].reshape(block, channels)
    width = channels >> bits
    row = lax.broadcasted_iota(jnp.int32, out.shape[:1] + (channels,), 0)
    chan = core * width + row
    for place in range(bits - 1):
        low = width << (bits - 2 - place)
        own = (me >> (place + 1)) & 1
        late = lax.rem(row, 2 * low) >= low
        chan = chan - jnp.where(late, low, 0)
        bit = jnp.where(late, own, 1 - own)
        chan = chan + bit * (width << (place + 1))
    index = lax.broadcasted_iota(jnp.int32, chan.shape, 1)
    table = (index == chan).astype(F32).astype(BF16)
    out[...] = lax.dot_general(
        table, rows[...], (((1,), (1,)), ((), ())), preferred_element_type=F32
    ).astype(BF16)


def tap_block(mid, side, t, start, rows):
    at = pl.ds(start, rows)
    return mid[at, :] if t % 3 == 1 else side[(t % 3) // 2, at, :]


def halves(value, part):
    taps = value.shape[1] // (2 * part)
    low = [value[:, 2 * t * part : (2 * t + 1) * part] for t in range(taps)]
    high = [value[:, (2 * t + 1) * part : (2 * t + 2) * part] for t in range(taps)]
    return jnp.concatenate(low, axis=1), jnp.concatenate(high, axis=1)


def second_bit(value):
    quarter = value.shape[0] // 4
    one, two, three, four = [value[k * quarter : (k + 1) * quarter] for k in range(4)]
    return jnp.concatenate([one, three]), jnp.concatenate([two, four])


def grad_kernel(block, by_dp, info, lhs, mid, side, *refs):
    outs, stages, sem = refs[:4], refs[4:8], refs[8]
    channels = mid.shape[1]
    copies = []
    for group, cut, base in ((GROUP_A, False, 0), (GROUP_B, by_dp, 2)):
        for first in range(0, len(group), 2):
            pair = group[first : first + 2]
            rhs = [tap_block(mid, side, t, (t // 3) * block, lhs.shape[1]) for t in pair]
            rhs = rhs[0] if len(rhs) == 1 else jnp.concatenate(rhs, axis=1)
            got = jnp.dot(lhs[...], rhs, preferred_element_type=F32)
            if cut:
                low, high = halves(got, channels // 2)
                sent = jnp.where(info[3] == 0, high, low)
                kept = jnp.where(info[3] == 0, low, high)
                start = first * channels // 2
            else:
                sent, kept = second_bit(got)
                start = first * channels
            at = slice(start, start + sent.shape[1])
            stages[base][:, at] = sent.astype(BF16)
            stages[base + 1][:, at] = kept
            for k in (base, base + 1):
                copy = pltpu.make_async_copy(
                    stages[k].at[:, at], outs[k].at[:, at], sem.at[len(copies)]
                )
                copy.start()
                copies.append(copy)
    for copy in copies:
        copy.wait()


def fold_kernel(kept, got, sent_out, kept_out):
    cut = sent_out.shape[0]
    sent_out[...] = (kept[:cut] + got[:cut].astype(F32)).astype(BF16)
    kept_out[...] = kept[cut:] + got[cut:].astype(F32)


def fold_second_kernel(kept, got, sent_out, kept_out):
    sent, own = second_bit(kept[...] + got[...].astype(F32))
    sent_out[...] = sent.astype(BF16)
    kept_out[...] = own


def part_kernel(part, info, kept, got, sent_out, kept_out):
    low, high = halves(kept[...] + got[...].astype(F32), part)
    sent_out[...] = jnp.where(info[3] == 0, high, low).astype(BF16)
    kept_out[...] = jnp.where(info[3] == 0, low, high)


def conv_kernel(info, places, mid, *refs):
    parts, (x, out, w, side, total, sem) = refs[:-6], refs[-6:]
    images, _, columns, channels = x.shape
    block = images * columns
    taps = w.shape[0]
    own = pl.multiple_of(2 * info[0] * block, 64)
    copies = [
        [
            pltpu.make_async_copy(
                part.at[t],
                w.at[t, pl.ds(pl.multiple_of(places[k], 32), part.shape[1]), :],
                sem.at[t, k],
            )
            for k, part in enumerate(parts)
        ]
        for t in range(taps)
    ]
    for tap in copies:
        for c in tap:
            c.start()

    def fill(k, carry):
        at = pl.multiple_of(k * columns, columns)
        down, up = shifted(mid[pl.ds(own + at, columns), :].astype(F32))
        side[0, pl.ds(at, columns), :] = down.astype(BF16)
        side[1, pl.ds(at, columns), :] = up.astype(BF16)
        return carry

    lax.fori_loop(0, 4 * images, fill, 0)
    for pair in (range(0, 2), range(2, 4), range(4, taps)):
        first = pair[0]
        for t in pair:
            for c in copies[t]:
                c.wait()
        rhs = w[first : first + len(pair)].reshape(len(pair) * channels, channels)
        for r in range(2):
            lhs = []
            for t in pair:
                at = (r + t // 3) * block
                if t % 3 == 1:
                    lhs.append(mid[pl.ds(pl.multiple_of(own + at, 64), block), :])
                else:
                    lhs.append(side[(t % 3) // 2, at : at + block, :])
            got = jnp.dot(jnp.concatenate(lhs, axis=1), rhs, preferred_element_type=F32)
            at = slice(r * block, (r + 1) * block)
            if first == 0:
                total[at] = got
            elif pair[-1] + 1 < taps:
                total[at] += got
            else:
                value = (total[at] + got).reshape(images, columns, channels)
                out[:, r] = (x[:, r].astype(F32) + value).astype(BF16)


def back_kernel(info, u, u_mate, rim, w, x, mean, rstd, gain, bias, out, sums, part, one, two):
    images, _, columns, channels = x.shape
    block = images * columns
    taps = w.shape[0]
    core = info[0]

    def fill(load, row):
        def step(img, carry):
            value = load(img)
            down, up = shifted(value.astype(F32))
            at = pl.ds(pl.multiple_of((row * images + img) * columns, columns), columns)
            part[0, at, :] = down.astype(BF16)
            part[1, at, :] = value
            part[2, at, :] = up.astype(BF16)
            return carry

        lax.fori_loop(0, images, step, 0)

    fill(lambda img: u[img, 0], 1)
    fill(lambda img: u[img, 1], 2)
    fill(lambda img: u_mate[img, core], 3 - 3 * core)
    fill(lambda img: rim[img], 3 * core)

    rhs = jnp.concatenate([w[t] for t in range(taps)], axis=1)
    for r in range(2):
        lhs = jnp.concatenate([
            part[2 - t % 3, (r + 2 - t // 3) * block : (r + 3 - t // 3) * block, :]
            for t in range(taps)
        ], axis=1)
        out[:, r] = lax.dot_general(
            lhs, rhs, (((1,), (1,)), ((), ())), preferred_element_type=F32
        ).reshape(images, columns, channels)

    def finish(img, carry):
        first = jnp.zeros((1, channels), F32)
        second = jnp.zeros((1, channels), F32)
        for r in range(2):
            centred = (x[img, r].astype(F32) - mean[pl.ds(img, 1), :]) * rstd[pl.ds(img, 1), :]
            normed = centred * gain[...] + bias[...]
            s = 1.0 / (1.0 + jnp.exp(-normed))
            grad = out[img, r] * s * (1.0 + normed * (1.0 - s))
            out[img, r] = grad
            first = first + jnp.sum(grad, axis=0, keepdims=True)
            second = second + jnp.sum(grad * centred, axis=0, keepdims=True)
        one[pl.ds(img, 1), :] = first
        two[pl.ds(img, 1), :] = second
        return carry

    lax.fori_loop(0, images, finish, 0)
    groups = channels // GSIZE
    member = members(channels, groups)
    sums[...] = jnp.zeros_like(sums)
    sums[0:images, 0:groups] = to_groups(one[...] * gain[...], member)
    sums[0:images, groups : 2 * groups] = to_groups(two[...] * gain[...], member)
    base = images + images % 2
    rows = channels // LANES
    gain_part = jnp.sum(two[...], axis=0, keepdims=True)
    bias_part = jnp.sum(one[...], axis=0, keepdims=True)
    for k in range(rows):
        at = slice(k * LANES, (k + 1) * LANES)
        sums[base + k : base + k + 1, :] = gain_part[:, at]
        sums[base + rows + k : base + rows + k + 1, :] = bias_part[:, at]


def input_kernel(size, sums, grad, x, u, mean, rstd, gain, out):
    images, rows, columns, channels = x.shape
    groups = channels // GSIZE
    member = members(channels, groups)
    means = sums[...] / size
    first = to_chans(means[:images, :groups], member)
    second = to_chans(means[:images, groups : 2 * groups], member)
    for img in range(images):
        at = slice(img, img + 1)
        for r in range(rows):
            centred = (x[img, r].astype(F32) - mean[at]) * rstd[at]
            inner = grad[img, r] * gain[...] - first[at] - centred * second[at]
            out[img, r] = (u[img, r].astype(F32) + rstd[at] * inner).astype(BF16)


def body(inputs, norm_gain, norm_bias, conv_weight, upstream):
    images, rows, columns, channels = inputs.shape
    count, dps = lax.axis_size("space"), lax.axis_size("dp")
    me, half = lax.axis_index("space"), lax.axis_index("dp")
    core, mate = me & 1, me ^ 1
    groups = channels // GSIZE
    bits = count.bit_length() - 1
    size = float(rows * columns * GSIZE * count)
    block = images * columns
    two = dps == 2
    gain_row, bias_row = norm_gain[None], norm_bias[None]
    taps = conv_weight.shape[0]
    own_ok = jnp.where((me == 0) | (me == count - 1), 0, 1)
    mate_ok = jnp.where((mate == 0) | (mate == count - 1), 0, 1)
    info = jnp.stack(
        [core, own_ok, mate_ok, half if two else 0 * core, me]
    ).astype(jnp.int32)

    pairs = []
    for i in range(1, count - 1, 2):
        pairs += [(i, i + 1), (i + 1, i)]
    x_mate = swap(inputs, "space", 1)
    u_mate = swap(upstream, "space", 1)

    part = conv_weight.shape[1] // 2
    row_shape = (images, columns, channels)
    out_shape = [struct((2 * images, groups), F32), struct(row_shape, BF16), struct(row_shape, BF16)]
    operands = [info, inputs, in_hbm(upstream)]
    if two:
        out_shape.append(struct((taps, part, channels), BF16))
        operands.append(in_hbm(conv_weight))
    stats, edge_x, edge_u, *w_sent = kernel_call(
        stats_kernel, 16, tuple(out_shape), [S, V, H] + [H] * (len(operands) - 3), "stats",
        [pltpu.SemaphoreType.DMA((3,))],
    )(*operands)
    if two:
        w_low = swap(w_sent[0], "dp", 1)
    rim_x = lax.ppermute(edge_x, "space", pairs)
    lhs = kernel_call(
        functools.partial(turn_kernel, bits), 16, struct((channels // 2, 4 * block), BF16),
        [S, V, V], "turn", [pltpu.VMEM((4 * block, channels), BF16)],
    )(info, upstream, u_mate)
    for place in [0] + list(range(2, bits)) + [1]:
        if place == 1:
            stats, rim_x, lhs = lax.optimization_barrier((stats, rim_x, lhs))
        stats = stats + swap(stats, "space", 1 << place)
    rim_x_mate = swap(rim_x, "space", 1)
    rim_u = lax.ppermute(after(edge_u, stats), "space", pairs)

    act_mid, act_side, mean, rstd = kernel_call(
        functools.partial(act_kernel, size), 24,
        (
            struct((6 * block, channels), BF16),
            struct((2, 6 * block, channels), BF16),
            struct((images, channels), F32),
            struct((images, channels), F32),
        ),
        [S] + [V] * 7, "activate",
    )(info, stats, inputs, x_mate, rim_x, rim_x_mate, gain_row, bias_row)

    def fold(kept, got, kernel=fold_kernel):
        shape = (kept.shape[0] // 2, kept.shape[1])
        return kernel_call(
            kernel, 8, (struct(shape, BF16), struct(shape, F32)), [V, V], "fold"
        )(kept, got)

    def split(kept, got):
        shape = (kept.shape[0], kept.shape[1] // 2)
        return kernel_call(
            functools.partial(part_kernel, channels // 2), 8,
            (struct(shape, BF16), struct(shape, F32)), [S, V, V], "split",
        )(info, kept, got)

    width_a, width_b = len(GROUP_A) * channels, len(GROUP_B) * channels
    shape_b = (channels // 2, width_b // 2) if two else (channels // 4, width_b)
    shapes = [((channels // 4, width_a), BF16), ((channels // 4, width_a), F32)]
    shapes += [(shape_b, BF16), (shape_b, F32)]
    sent_a, kept_a, sent_b, kept_b = kernel_call(
        functools.partial(grad_kernel, block, two), 28,
        tuple(pltpu.HBM(*shape) for shape in shapes), [S] + [V] * 3, "weight_terms",
        [pltpu.VMEM(*shape) for shape in shapes] + [pltpu.SemaphoreType.DMA((10,))], (H,) * 4,
    )(info, lhs, act_mid, act_side)
    got_a = swap(sent_a, "space", 4)
    got_b = swap(sent_b, "dp", 1) if two else swap(sent_b, "space", 4)

    if two:
        w_low = after(w_low, sent_b)
        other = (1 - half) * 2 * part
        spots = jnp.stack([half * 2 * part, other + core * part, other + (1 - core) * part])
        w_parts = [conv_weight, w_low, swap(w_low, "space", 1)]
    else:
        spots = jnp.zeros((1,), jnp.int32)
        w_parts = [lax.all_gather(conv_weight, "dp", axis=1, tiled=True)]
    mixed, weights = kernel_call(
        conv_kernel, 32,
        (struct(inputs.shape, BF16), struct((taps, channels, channels), BF16)),
        [S, S, V] + [H] * len(w_parts) + [V], "conv_forward",
        [
            pltpu.VMEM((2, 4 * block, channels), BF16),
            pltpu.VMEM((2 * block, channels), F32),
            pltpu.SemaphoreType.DMA((taps, len(w_parts))),
        ],
    )(
        after(info, sent_b), spots.astype(jnp.int32), act_mid,
        *[in_hbm(value) for value in w_parts], inputs,
    )

    sent_a, kept_a = fold(kept_a, after(got_a, mixed))
    got_a = swap(sent_a, "space", 2)
    got_b = after(got_b, sent_a)
    sent_b, kept_b = fold(kept_b, got_b, fold_second_kernel if two else fold_kernel)
    got_b = swap(sent_b, "space", 4 if two else 2)

    grad, sums = kernel_call(
        back_kernel, 32,
        (struct(inputs.shape, F32), struct((40, LANES), F32)), [S] + [V] * 9, "conv_backward",
        [
            pltpu.VMEM((3, 4 * block, channels), BF16),
            pltpu.VMEM((images, channels), F32),
            pltpu.VMEM((images, channels), F32),
        ],
    )(
        after(info, sent_a, sent_b), upstream, u_mate, rim_u, weights, inputs, mean, rstd,
        gain_row, bias_row,
    )

    if two:
        sent_a, kept_a = split(kept_a, after(got_a, sums))
        got_a = swap(sent_a, "dp", 1)
        sent_b, kept_b = fold(kept_b, after(got_b, sent_a))
        got_b = swap(sent_b, "space", 2)
        sums = after(sums, sent_b)
    for place in [0] + list(range(2, bits)) + [1]:
        sums = sums + swap(sums, "space", 1 << place)
    sent_a, kept_a = fold(kept_a, after(got_a, sums))
    got_a = swap(sent_a, "space", 8)
    sent_b, kept_b = fold(kept_b, after(got_b, sent_a))
    got_b = swap(sent_b, "space", 8)
    sums = after(sums, sent_b)
    input_grad = kernel_call(
        functools.partial(input_kernel, size), 16, struct(inputs.shape, BF16), [V] * 7, "input_grad"
    )(sums, grad, inputs, upstream, mean, rstd, gain_row)

    base = images + images % 2
    totals = sums[base : base + 2 * channels // LANES]
    totals = totals + after(swap(totals, "dp", 1), input_grad) if two else lax.psum(totals, "dp")
    totals = totals.reshape(2, channels)

    got_a = after(got_a, input_grad)
    weight_grad = jnp.concatenate(
        [kept_a + got_a.astype(F32), kept_b + got_b.astype(F32)], axis=1
    )
    weight_grad = weight_grad.reshape(weight_grad.shape[0], taps, -1)
    if not two:
        weight_grad = lax.psum_scatter(weight_grad, "dp", scatter_dimension=2, tiled=True)
    weight_grad = weight_grad.transpose(1, 2, 0)
    return (mixed, input_grad, weight_grad, totals[0], totals[1])


def solution(mesh):
    in_specs = (
        P("dp", "space", None, None),
        P(),
        P(),
        P(None, "dp", None),
        P("dp", "space", None, None),
    )
    out_specs = (
        P("dp", "space", None, None),
        P("dp", "space", None, None),
        P(None, "dp", "space"),
        P(),
        P(),
    )
    return jax.shard_map(body, mesh=mesh, in_specs=in_specs, out_specs=out_specs, check_vma=False)
```

```python
import functools

import jax
import jax.numpy as jnp
from jax import lax
from jax.experimental import pallas as pl
from jax.experimental.pallas import tpu as pltpu
from jax.sharding import PartitionSpec as P

GSIZE = 40
EPS = 1e-05
GROUP_A, GROUP_B = (0, 1, 2, 3), (4, 5, 6, 7, 8)
LANES = 128
F32 = jnp.float32
BF16 = jnp.bfloat16
HIGHEST = lax.Precision.HIGHEST
VMEM_SPEC = pl.BlockSpec(memory_space=pltpu.VMEM)
SMEM_SPEC = pl.BlockSpec(memory_space=pltpu.SMEM)
HBM_SPEC = pl.BlockSpec(memory_space=pltpu.HBM)
MIB = 1 << 20
V, S, H = VMEM_SPEC, SMEM_SPEC, HBM_SPEC


def kernel_call(body, mib, out_shape, in_specs, name, scratch=(), out_specs=None):
    return pl.pallas_call(
        body,
        out_shape=out_shape,
        in_specs=in_specs,
        out_specs=out_specs or jax.tree.map(lambda _: VMEM_SPEC, out_shape),
        scratch_shapes=scratch,
        compiler_params=pltpu.CompilerParams(vmem_limit_bytes=mib * MIB),
        name=name,
    )


def struct(shape, dtype):
    return jax.ShapeDtypeStruct(shape, dtype)


def swap(value, axis, bit):
    count = lax.axis_size(axis)
    return lax.ppermute(value, axis, [(i, i ^ bit) for i in range(count)])


def in_hbm(value):
    return pltpu.with_memory_space_constraint(value, pltpu.HBM)


def after(value, *others):
    return lax.optimization_barrier((value,) + others)[0]


def members(channels, groups):
    chan = lax.broadcasted_iota(jnp.int32, (groups, channels), 1)
    first = lax.broadcasted_iota(jnp.int32, (groups, channels), 0) * GSIZE
    return ((chan >= first) & (chan < first + GSIZE)).astype(F32)


def to_groups(sums, member):
    return lax.dot_general(
        sums, member, (((1,), (1,)), ((), ())), precision=HIGHEST, preferred_element_type=F32
    )


def to_chans(values, member):
    return jnp.dot(values, member, precision=HIGHEST, preferred_element_type=F32)


def shifted(block):
    columns = block.shape[0]
    col = lax.broadcasted_iota(jnp.int32, block.shape, 0)
    down = jnp.where(col == 0, 0.0, pltpu.roll(block, 1, axis=0))
    up = jnp.where(col == columns - 1, 0.0, pltpu.roll(block, columns - 1, axis=0))
    return down, up


def stats_kernel(info, x, u, *refs):
    if len(refs) == 6:
        w, out, edge_x, edge_u, w_sent, sem = refs
    else:
        out, edge_x, edge_u, sem = refs
    images, _, _, channels = x.shape
    core = info[0]
    copies = [
        pltpu.make_async_copy(x.at[:, core], edge_x, sem.at[0]),
        pltpu.make_async_copy(u.at[:, core], edge_u, sem.at[1]),
    ]
    if len(refs) == 6:
        rows = w_sent.shape[1]
        at = pl.ds(pl.multiple_of(core * rows, 32), rows)
        copies.append(pltpu.make_async_copy(w.at[:, at, :], w_sent, sem.at[2]))
    for c in copies:
        c.start()
    one, two = [], []
    for img in range(images):
        value = x[img].astype(F32).reshape(-1, channels)
        one.append(jnp.sum(value, axis=0, keepdims=True))
        two.append(jnp.sum(value * value, axis=0, keepdims=True))
    out[...] = to_groups(jnp.concatenate(one + two), members(channels, channels // GSIZE))
    for c in copies:
        c.wait()


def act_kernel(size, info, stats, x, x_mate, rim, rim_mate, gain, bias, mid, side, mean, rstd):
    images, _, columns, channels = x.shape
    core, own_ok, mate_ok = info[0], info[1], info[2]
    member = members(channels, channels // GSIZE)
    group_mean = stats[:images] / size
    group_rstd = lax.rsqrt(stats[images:] / size - group_mean * group_mean + EPS)
    mean[...] = to_chans(group_mean, member)
    rstd[...] = to_chans(group_rstd, member)

    def fill(load, row, keep):
        def step(img, carry):
            value = load(img).astype(F32)
            scale = rstd[pl.ds(img, 1), :] * gain[...]
            normed = (value - mean[pl.ds(img, 1), :]) * scale + bias[...]
            act = normed / (1.0 + jnp.exp(-normed))
            if keep is not None:
                act = jnp.where(keep > 0, act, 0.0)
            down, up = shifted(act)
            at = pl.ds(pl.multiple_of((row * images + img) * columns, columns), columns)
            mid[at, :] = act.astype(BF16)
            side[0, at, :] = down.astype(BF16)
            side[1, at, :] = up.astype(BF16)
            return carry

        lax.fori_loop(0, images, step, 0)

    fill(lambda img: x[img, 0], 1 + 2 * core, None)
    fill(lambda img: x[img, 1], 2 + 2 * core, None)
    fill(lambda img: x_mate[img, 0], 3 - 2 * core, None)
    fill(lambda img: x_mate[img, 1], 4 - 2 * core, None)
    fill(lambda img: rim[img], 5 * core, own_ok)
    fill(lambda img: rim_mate[img], 5 - 5 * core, mate_ok)


def turn_kernel(bits, info, u, u_mate, out, rows):
    images, _, columns, channels = u.shape
    core, me = info[0], info[4]
    block = images * columns
    for r in range(2):
        at = pl.multiple_of((r + 2 * core) * block, 64)
        rows[pl.ds(at, block), :] = u[:, r].reshape(block, channels)
        at = pl.multiple_of((r + 2 - 2 * core) * block, 64)
        rows[pl.ds(at, block), :] = u_mate[:, r].reshape(block, channels)
    width = channels >> bits
    row = lax.broadcasted_iota(jnp.int32, out.shape[:1] + (channels,), 0)
    chan = core * width + row
    for place in range(bits - 1):
        low = width << (bits - 2 - place)
        own = (me >> (place + 1)) & 1
        late = lax.rem(row, 2 * low) >= low
        chan = chan - jnp.where(late, low, 0)
        bit = jnp.where(late, own, 1 - own)
        chan = chan + bit * (width << (place + 1))
    index = lax.broadcasted_iota(jnp.int32, chan.shape, 1)
    table = (index == chan).astype(F32).astype(BF16)
    out[...] = lax.dot_general(
        table, rows[...], (((1,), (1,)), ((), ())), preferred_element_type=F32
    ).astype(BF16)


def tap_block(mid, side, t, start, rows):
    at = pl.ds(start, rows)
    return mid[at, :] if t % 3 == 1 else side[(t % 3) // 2, at, :]


def halves(value, part):
    taps = value.shape[1] // (2 * part)
    low = [value[:, 2 * t * part : (2 * t + 1) * part] for t in range(taps)]
    high = [value[:, (2 * t + 1) * part : (2 * t + 2) * part] for t in range(taps)]
    return jnp.concatenate(low, axis=1), jnp.concatenate(high, axis=1)


def second_bit(value):
    quarter = value.shape[0] // 4
    one, two, three, four = [value[k * quarter : (k + 1) * quarter] for k in range(4)]
    return jnp.concatenate([one, three]), jnp.concatenate([two, four])


def grad_kernel(block, by_dp, info, lhs, mid, side, *refs):
    outs, stages, sem = refs[:4], refs[4:8], refs[8]
    channels = mid.shape[1]
    copies = []
    for group, cut, base in ((GROUP_A, False, 0), (GROUP_B, by_dp, 2)):
        for first in range(0, len(group), 2):
            pair = group[first : first + 2]
            rhs = [tap_block(mid, side, t, (t // 3) * block, lhs.shape[1]) for t in pair]
            rhs = rhs[0] if len(rhs) == 1 else jnp.concatenate(rhs, axis=1)
            got = jnp.dot(lhs[...], rhs, preferred_element_type=F32)
            if cut:
                low, high = halves(got, channels // 2)
                sent = jnp.where(info[3] == 0, high, low)
                kept = jnp.where(info[3] == 0, low, high)
                start = first * channels // 2
            else:
                sent, kept = second_bit(got)
                start = first * channels
            at = slice(start, start + sent.shape[1])
            stages[base][:, at] = sent.astype(BF16)
            stages[base + 1][:, at] = kept
            for k in (base, base + 1):
                copy = pltpu.make_async_copy(
                    stages[k].at[:, at], outs[k].at[:, at], sem.at[len(copies)]
                )
                copy.start()
                copies.append(copy)
    for copy in copies:
        copy.wait()


def fold_kernel(kept, got, sent_out, kept_out):
    cut = sent_out.shape[0]
    sent_out[...] = (kept[:cut] + got[:cut].astype(F32)).astype(BF16)
    kept_out[...] = kept[cut:] + got[cut:].astype(F32)


def part_kernel(part, info, kept, got, sent_out, kept_out):
    low, high = halves(kept[...] + got[...].astype(F32), part)
    sent_out[...] = jnp.where(info[3] == 0, high, low).astype(BF16)
    kept_out[...] = jnp.where(info[3] == 0, low, high)


def conv_kernel(info, mid, w, x, out, side):
    images, _, columns, channels = x.shape
    block = images * columns
    first = pl.multiple_of(2 * info[0] * block, 64)
    taps = w.shape[0]

    def fill(k, carry):
        at = pl.multiple_of(k * columns, columns)
        down, up = shifted(mid[pl.ds(first + at, columns), :].astype(F32))
        side[0, pl.ds(at, columns), :] = down.astype(BF16)
        side[1, pl.ds(at, columns), :] = up.astype(BF16)
        return carry

    lax.fori_loop(0, 4 * images, fill, 0)
    rhs = w[...].reshape(taps * channels, channels)
    for r in range(2):
        lhs = []
        for t in range(taps):
            at = (r + t // 3) * block
            if t % 3 == 1:
                lhs.append(mid[pl.ds(pl.multiple_of(first + at, 64), block), :])
            else:
                lhs.append(side[(t % 3) // 2, at : at + block, :])
        value = jnp.dot(jnp.concatenate(lhs, axis=1), rhs, preferred_element_type=F32)
        value = value.reshape(images, columns, channels)
        out[:, r] = (x[:, r].astype(F32) + value).astype(BF16)


def back_kernel(info, places, *refs):
    u, u_mate, rim, x, mean, rstd, gain, bias, out, sums, w, part, one, two, sem = refs[-15:]
    pieces = refs[:-15]
    images, _, columns, channels = x.shape
    block = images * columns
    taps = w.shape[0]
    core = info[0]
    copies = [
        [
            pltpu.make_async_copy(
                piece.at[t],
                w.at[t, pl.ds(pl.multiple_of(places[k], 32), piece.shape[1]), :],
                sem.at[t, k],
            )
            for k, piece in enumerate(pieces)
        ]
        for t in range(taps)
    ]
    for tap in copies:
        for c in tap:
            c.start()

    def fill(load, row):
        def step(img, carry):
            value = load(img)
            down, up = shifted(value.astype(F32))
            at = pl.ds(pl.multiple_of((row * images + img) * columns, columns), columns)
            part[0, at, :] = down.astype(BF16)
            part[1, at, :] = value
            part[2, at, :] = up.astype(BF16)
            return carry

        lax.fori_loop(0, images, step, 0)

    fill(lambda img: u[img, 0], 1)
    fill(lambda img: u[img, 1], 2)
    fill(lambda img: u_mate[img, core], 3 - 3 * core)
    fill(lambda img: rim[img], 3 * core)

    for group in (range(0, 4), range(4, taps)):
        for t in group:
            for c in copies[t]:
                c.wait()
        rhs = jnp.concatenate([w[t] for t in group], axis=1)
        for r in range(2):
            lhs = jnp.concatenate([
                part[2 - t % 3, (r + 2 - t // 3) * block : (r + 3 - t // 3) * block, :]
                for t in group
            ], axis=1)
            value = lax.dot_general(
                lhs, rhs, (((1,), (1,)), ((), ())), preferred_element_type=F32
            ).reshape(images, columns, channels)
            if group[0] == 0:
                out[:, r] = value
            else:
                out[:, r] += value

    def finish(img, carry):
        first = jnp.zeros((1, channels), F32)
        second = jnp.zeros((1, channels), F32)
        for r in range(2):
            centred = (x[img, r].astype(F32) - mean[pl.ds(img, 1), :]) * rstd[pl.ds(img, 1), :]
            normed = centred * gain[...] + bias[...]
            s = 1.0 / (1.0 + jnp.exp(-normed))
            grad = out[img, r] * s * (1.0 + normed * (1.0 - s))
            out[img, r] = grad
            first = first + jnp.sum(grad, axis=0, keepdims=True)
            second = second + jnp.sum(grad * centred, axis=0, keepdims=True)
        one[pl.ds(img, 1), :] = first
        two[pl.ds(img, 1), :] = second
        return carry

    lax.fori_loop(0, images, finish, 0)
    groups = channels // GSIZE
    member = members(channels, groups)
    sums[...] = jnp.zeros_like(sums)
    sums[0:images, 0:groups] = to_groups(one[...] * gain[...], member)
    sums[0:images, groups : 2 * groups] = to_groups(two[...] * gain[...], member)
    base = images + images % 2
    rows = channels // LANES
    gain_part = jnp.sum(two[...], axis=0, keepdims=True)
    bias_part = jnp.sum(one[...], axis=0, keepdims=True)
    for k in range(rows):
        at = slice(k * LANES, (k + 1) * LANES)
        sums[base + k : base + k + 1, :] = gain_part[:, at]
        sums[base + rows + k : base + rows + k + 1, :] = bias_part[:, at]


def input_kernel(size, sums, grad, x, u, mean, rstd, gain, out):
    images, rows, columns, channels = x.shape
    groups = channels // GSIZE
    member = members(channels, groups)
    means = sums[...] / size
    first = to_chans(means[:images, :groups], member)
    second = to_chans(means[:images, groups : 2 * groups], member)
    for img in range(images):
        at = slice(img, img + 1)
        for r in range(rows):
            centred = (x[img, r].astype(F32) - mean[at]) * rstd[at]
            inner = grad[img, r] * gain[...] - first[at] - centred * second[at]
            out[img, r] = (u[img, r].astype(F32) + rstd[at] * inner).astype(BF16)


def body(inputs, norm_gain, norm_bias, conv_weight, upstream):
    images, rows, columns, channels = inputs.shape
    count, dps = lax.axis_size("space"), lax.axis_size("dp")
    me, half = lax.axis_index("space"), lax.axis_index("dp")
    core, mate = me & 1, me ^ 1
    groups = channels // GSIZE
    bits = count.bit_length() - 1
    size = float(rows * columns * GSIZE * count)
    block = images * columns
    two = dps == 2
    gain_row, bias_row = norm_gain[None], norm_bias[None]
    taps = conv_weight.shape[0]
    own_ok = jnp.where((me == 0) | (me == count - 1), 0, 1)
    mate_ok = jnp.where((mate == 0) | (mate == count - 1), 0, 1)
    info = jnp.stack(
        [core, own_ok, mate_ok, half if two else 0 * core, me]
    ).astype(jnp.int32)

    pairs = []
    for i in range(1, count - 1, 2):
        pairs += [(i, i + 1), (i + 1, i)]
    x_mate = swap(inputs, "space", 1)
    u_mate = swap(upstream, "space", 1)

    part = conv_weight.shape[1] // 2
    row_shape = (images, columns, channels)
    out_shape = [struct((2 * images, groups), F32), struct(row_shape, BF16), struct(row_shape, BF16)]
    operands = [info, inputs, in_hbm(upstream)]
    if two:
        out_shape.append(struct((taps, part, channels), BF16))
        operands.append(in_hbm(conv_weight))
    stats, edge_x, edge_u, *w_sent = kernel_call(
        stats_kernel, 16, tuple(out_shape), [S, V, H] + [H] * (len(operands) - 3), "stats",
        [pltpu.SemaphoreType.DMA((3,))],
    )(*operands)
    if two:
        w_low = swap(w_sent[0], "dp", 1)
    rim_x = lax.ppermute(edge_x, "space", pairs)
    lhs = kernel_call(
        functools.partial(turn_kernel, bits), 16, struct((channels // 2, 4 * block), BF16),
        [S, V, V], "turn", [pltpu.VMEM((4 * block, channels), BF16)],
    )(info, upstream, u_mate)
    for place in [0] + list(range(2, bits)) + [1]:
        if place == 1:
            stats, rim_x, lhs = lax.optimization_barrier((stats, rim_x, lhs))
        stats = stats + swap(stats, "space", 1 << place)
    rim_x_mate = swap(rim_x, "space", 1)
    rim_u = lax.ppermute(after(edge_u, stats), "space", pairs)

    act_mid, act_side, mean, rstd = kernel_call(
        functools.partial(act_kernel, size), 24,
        (
            struct((6 * block, channels), BF16),
            struct((2, 6 * block, channels), BF16),
            struct((images, channels), F32),
            struct((images, channels), F32),
        ),
        [S] + [V] * 7, "activate",
    )(info, stats, inputs, x_mate, rim_x, rim_x_mate, gain_row, bias_row)

    def fold(kept, got):
        shape = (kept.shape[0] // 2, kept.shape[1])
        return kernel_call(
            fold_kernel, 8, (struct(shape, BF16), struct(shape, F32)), [V, V], "fold"
        )(kept, got)

    def split(kept, got):
        shape = (kept.shape[0], kept.shape[1] // 2)
        return kernel_call(
            functools.partial(part_kernel, channels // 2), 8,
            (struct(shape, BF16), struct(shape, F32)), [S, V, V], "split",
        )(info, kept, got)

    width_a, width_b = len(GROUP_A) * channels, len(GROUP_B) * channels
    shape_b = (channels // 2, width_b // 2) if two else (channels // 4, width_b)
    shapes = [((channels // 4, width_a), BF16), ((channels // 4, width_a), F32)]
    shapes += [(shape_b, BF16), (shape_b, F32)]
    sent_a, kept_a, sent_b, kept_b = kernel_call(
        functools.partial(grad_kernel, block, two), 28,
        tuple(pltpu.HBM(*shape) for shape in shapes), [S] + [V] * 3, "weight_terms",
        [pltpu.VMEM(*shape) for shape in shapes] + [pltpu.SemaphoreType.DMA((10,))], (H,) * 4,
    )(info, lhs, act_mid, act_side)
    sent_a, sent_b, rim_u = lax.optimization_barrier((sent_a, sent_b, rim_u))
    got_a = swap(sent_a, "space", 4)
    got_b = swap(sent_b, "dp", 1) if two else swap(sent_b, "space", 4)

    if two:
        w_low = after(w_low, sent_b)
        other = (1 - half) * 2 * part
        spots = jnp.stack([half * 2 * part, other + core * part, other + (1 - core) * part])
        w_parts = [conv_weight, w_low, swap(w_low, "space", 1)]
    else:
        spots = jnp.zeros((1,), jnp.int32)
        w_parts = [lax.all_gather(conv_weight, "dp", axis=1, tiled=True)]
    grad, sums, weights = kernel_call(
        back_kernel, 32,
        (
            struct(inputs.shape, F32),
            struct((40, LANES), F32),
            struct((taps, channels, channels), BF16),
        ),
        [S, S] + [H] * len(w_parts) + [V] * 8, "conv_backward",
        [
            pltpu.VMEM((3, 4 * block, channels), BF16),
            pltpu.VMEM((images, channels), F32),
            pltpu.VMEM((images, channels), F32),
            pltpu.SemaphoreType.DMA((taps, len(w_parts))),
        ],
    )(
        after(info, sent_b), spots.astype(jnp.int32), *[in_hbm(value) for value in w_parts],
        upstream, u_mate, rim_u, inputs, mean, rstd, gain_row, bias_row,
    )

    base = images + images % 2
    last = base + 2 * channels // LANES
    totals = sums[base:last]
    if two:
        sent_a, kept_a = split(kept_a, after(got_a, sums))
        got_a = swap(sent_a, "dp", 1)
        sent_b, kept_b = fold(kept_b, after(got_b, sent_a))
        got_b = swap(sent_b, "space", 2)
        totals = totals + after(swap(totals, "dp", 1), sent_b)
    else:
        totals = lax.psum(totals, "dp")
    sums = jnp.concatenate([sums[:base], totals, sums[last:]])
    for place in [0] + list(range(2, bits)):
        sums = sums + swap(sums, "space", 1 << place)
    sent_a, kept_a = fold(kept_a, after(got_a, sums))
    got_a = swap(sent_a, "space", 2)
    sent_b, kept_b = fold(kept_b, after(got_b, sent_a))
    got_b = swap(sent_b, "space", 4 if two else 2)
    sums = after(sums, sent_b)
    sums = sums + swap(sums, "space", 2)
    input_grad = kernel_call(
        functools.partial(input_kernel, size), 16, struct(inputs.shape, BF16), [V] * 7, "input_grad"
    )(sums, grad, inputs, upstream, mean, rstd, gain_row)
    totals = sums[base:last].reshape(2, channels)
    sent_a, kept_a = fold(kept_a, after(got_a, input_grad))
    got_a = swap(sent_a, "space", 8)
    sent_b, kept_b = fold(kept_b, after(got_b, sent_a))
    got_b = swap(sent_b, "space", 8)
    mixed = kernel_call(
        conv_kernel, 32, struct(inputs.shape, BF16), [S] + [V] * 3, "conv_forward",
        [pltpu.VMEM((2, 4 * block, channels), BF16)],
    )(after(info, sent_b), act_mid, weights, inputs)
    got_a = after(got_a, mixed)
    weight_grad = jnp.concatenate(
        [kept_a + got_a.astype(F32), kept_b + got_b.astype(F32)], axis=1
    )
    weight_grad = weight_grad.reshape(weight_grad.shape[0], taps, -1)
    if not two:
        weight_grad = lax.psum_scatter(weight_grad, "dp", scatter_dimension=2, tiled=True)
    weight_grad = weight_grad.transpose(1, 2, 0)
    return (mixed, input_grad, weight_grad, totals[0], totals[1])


def solution(mesh):
    in_specs = (
        P("dp", "space", None, None),
        P(),
        P(),
        P(None, "dp", None),
        P("dp", "space", None, None),
    )
    out_specs = (
        P("dp", "space", None, None),
        P("dp", "space", None, None),
        P(None, "dp", "space"),
        P(),
        P(),
    )
    return jax.shard_map(body, mesh=mesh, in_specs=in_specs, out_specs=out_specs, check_vma=False)
```

```python
import functools

import jax
import jax.numpy as jnp
from jax import lax
from jax.experimental import pallas as pl
from jax.experimental.pallas import tpu as pltpu
from jax.sharding import PartitionSpec as P

GSIZE = 40
EPS = 1e-05
GROUP_A, GROUP_B = (0, 1, 2, 3, 4), (5, 6, 7, 8)
LANES = 128
F32 = jnp.float32
BF16 = jnp.bfloat16
HIGHEST = lax.Precision.HIGHEST
VMEM_SPEC = pl.BlockSpec(memory_space=pltpu.VMEM)
SMEM_SPEC = pl.BlockSpec(memory_space=pltpu.SMEM)
HBM_SPEC = pl.BlockSpec(memory_space=pltpu.HBM)
MIB = 1 << 20
V, S, H = VMEM_SPEC, SMEM_SPEC, HBM_SPEC


def kernel_call(body, mib, out_shape, in_specs, name, scratch=(), out_specs=None):
    return pl.pallas_call(
        body,
        out_shape=out_shape,
        in_specs=in_specs,
        out_specs=out_specs or jax.tree.map(lambda _: VMEM_SPEC, out_shape),
        scratch_shapes=scratch,
        compiler_params=pltpu.CompilerParams(vmem_limit_bytes=mib * MIB),
        name=name,
    )


def struct(shape, dtype):
    return jax.ShapeDtypeStruct(shape, dtype)


def swap(value, axis, bit):
    count = lax.axis_size(axis)
    return lax.ppermute(value, axis, [(i, i ^ bit) for i in range(count)])


def in_hbm(value):
    return pltpu.with_memory_space_constraint(value, pltpu.HBM)


def after(value, *others):
    return lax.optimization_barrier((value,) + others)[0]


def members(channels, groups):
    chan = lax.broadcasted_iota(jnp.int32, (groups, channels), 1)
    first = lax.broadcasted_iota(jnp.int32, (groups, channels), 0) * GSIZE
    return ((chan >= first) & (chan < first + GSIZE)).astype(F32)


def to_groups(sums, member):
    return lax.dot_general(
        sums, member, (((1,), (1,)), ((), ())), precision=HIGHEST, preferred_element_type=F32
    )


def to_chans(values, member):
    return jnp.dot(values, member, precision=HIGHEST, preferred_element_type=F32)


def shifted(block):
    columns = block.shape[0]
    col = lax.broadcasted_iota(jnp.int32, block.shape, 0)
    down = jnp.where(col == 0, 0.0, pltpu.roll(block, 1, axis=0))
    up = jnp.where(col == columns - 1, 0.0, pltpu.roll(block, columns - 1, axis=0))
    return down, up


def stats_kernel(info, x, u, *refs):
    if len(refs) == 6:
        w, out, edge_x, edge_u, w_sent, sem = refs
    else:
        out, edge_x, edge_u, sem = refs
    images, _, _, channels = x.shape
    core = info[0]
    copies = [
        pltpu.make_async_copy(x.at[:, core], edge_x, sem.at[0]),
        pltpu.make_async_copy(u.at[:, core], edge_u, sem.at[1]),
    ]
    if len(refs) == 6:
        rows = w_sent.shape[1]
        at = pl.ds(pl.multiple_of(core * rows, 32), rows)
        copies.append(pltpu.make_async_copy(w.at[:, at, :], w_sent, sem.at[2]))
    for c in copies:
        c.start()
    one, two = [], []
    for img in range(images):
        value = x[img].astype(F32).reshape(-1, channels)
        one.append(jnp.sum(value, axis=0, keepdims=True))
        two.append(jnp.sum(value * value, axis=0, keepdims=True))
    out[...] = to_groups(jnp.concatenate(one + two), members(channels, channels // GSIZE))
    for c in copies:
        c.wait()


def act_kernel(size, info, stats, x, x_mate, rim, rim_mate, gain, bias, mid, side, mean, rstd):
    images, _, columns, channels = x.shape
    core, own_ok, mate_ok = info[0], info[1], info[2]
    member = members(channels, channels // GSIZE)
    group_mean = stats[:images] / size
    group_rstd = lax.rsqrt(stats[images:] / size - group_mean * group_mean + EPS)
    mean[...] = to_chans(group_mean, member)
    rstd[...] = to_chans(group_rstd, member)

    def fill(load, row, keep):
        def step(img, carry):
            value = load(img).astype(F32)
            scale = rstd[pl.ds(img, 1), :] * gain[...]
            normed = (value - mean[pl.ds(img, 1), :]) * scale + bias[...]
            act = normed / (1.0 + jnp.exp(-normed))
            if keep is not None:
                act = jnp.where(keep > 0, act, 0.0)
            down, up = shifted(act)
            at = pl.ds(pl.multiple_of((row * images + img) * columns, columns), columns)
            mid[at, :] = act.astype(BF16)
            side[0, at, :] = down.astype(BF16)
            side[1, at, :] = up.astype(BF16)
            return carry

        lax.fori_loop(0, images, step, 0)

    fill(lambda img: x[img, 0], 1 + 2 * core, None)
    fill(lambda img: x[img, 1], 2 + 2 * core, None)
    fill(lambda img: x_mate[img, 0], 3 - 2 * core, None)
    fill(lambda img: x_mate[img, 1], 4 - 2 * core, None)
    fill(lambda img: rim[img], 5 * core, own_ok)
    fill(lambda img: rim_mate[img], 5 - 5 * core, mate_ok)


def turn_kernel(bits, info, u, u_mate, out, rows):
    images, _, columns, channels = u.shape
    core, me = info[0], info[4]
    block = images * columns
    for r in range(2):
        at = pl.multiple_of((r + 2 * core) * block, 64)
        rows[pl.ds(at, block), :] = u[:, r].reshape(block, channels)
        at = pl.multiple_of((r + 2 - 2 * core) * block, 64)
        rows[pl.ds(at, block), :] = u_mate[:, r].reshape(block, channels)
    width = channels >> bits
    row = lax.broadcasted_iota(jnp.int32, out.shape[:1] + (channels,), 0)
    chan = core * width + row
    for place in range(bits - 1):
        low = width << (bits - 2 - place)
        own = (me >> (place + 1)) & 1
        late = lax.rem(row, 2 * low) >= low
        chan = chan - jnp.where(late, low, 0)
        bit = jnp.where(late, own, 1 - own)
        chan = chan + bit * (width << (place + 1))
    index = lax.broadcasted_iota(jnp.int32, chan.shape, 1)
    table = (index == chan).astype(F32).astype(BF16)
    out[...] = lax.dot_general(
        table, rows[...], (((1,), (1,)), ((), ())), preferred_element_type=F32
    ).astype(BF16)


def tap_block(mid, side, t, start, rows):
    at = pl.ds(start, rows)
    return mid[at, :] if t % 3 == 1 else side[(t % 3) // 2, at, :]


def halves(value, part):
    taps = value.shape[1] // (2 * part)
    low = [value[:, 2 * t * part : (2 * t + 1) * part] for t in range(taps)]
    high = [value[:, (2 * t + 1) * part : (2 * t + 2) * part] for t in range(taps)]
    return jnp.concatenate(low, axis=1), jnp.concatenate(high, axis=1)


def second_bit(value):
    quarter = value.shape[0] // 4
    one, two, three, four = [value[k * quarter : (k + 1) * quarter] for k in range(4)]
    return jnp.concatenate([one, three]), jnp.concatenate([two, four])


def grad_kernel(block, by_dp, info, lhs, mid, side, *refs):
    outs, stages, sem = refs[:4], refs[4:8], refs[8]
    channels = mid.shape[1]
    copies = []
    for group, cut, base in ((GROUP_A, False, 0), (GROUP_B, by_dp, 2)):
        for first in range(0, len(group), 2):
            pair = group[first : first + 2]
            rhs = [tap_block(mid, side, t, (t // 3) * block, lhs.shape[1]) for t in pair]
            rhs = rhs[0] if len(rhs) == 1 else jnp.concatenate(rhs, axis=1)
            got = jnp.dot(lhs[...], rhs, preferred_element_type=F32)
            if cut:
                low, high = halves(got, channels // 2)
                sent = jnp.where(info[3] == 0, high, low)
                kept = jnp.where(info[3] == 0, low, high)
                start = first * channels // 2
            else:
                sent, kept = second_bit(got)
                start = first * channels
            at = slice(start, start + sent.shape[1])
            stages[base][:, at] = sent.astype(BF16)
            stages[base + 1][:, at] = kept
            for k in (base, base + 1):
                copy = pltpu.make_async_copy(
                    stages[k].at[:, at], outs[k].at[:, at], sem.at[len(copies)]
                )
                copy.start()
                copies.append(copy)
    for copy in copies:
        copy.wait()


def fold_kernel(kept, got, sent_out, kept_out):
    cut = sent_out.shape[0]
    sent_out[...] = (kept[:cut] + got[:cut].astype(F32)).astype(BF16)
    kept_out[...] = kept[cut:] + got[cut:].astype(F32)


def part_kernel(part, info, kept, got, sent_out, kept_out):
    low, high = halves(kept[...] + got[...].astype(F32), part)
    sent_out[...] = jnp.where(info[3] == 0, high, low).astype(BF16)
    kept_out[...] = jnp.where(info[3] == 0, low, high)


def last_kernel(kept_a, got_a, kept_b, got_b, out):
    part = out.shape[2]
    first = 0
    for kept, got in ((kept_a, got_a), (kept_b, got_b)):
        value = kept[...] + got[...].astype(F32)
        count = value.shape[1] // part
        for t in range(count):
            out[first + t] = value[:, t * part : (t + 1) * part]
        first += count


def conv_kernel(info, mid, w, x, out, side):
    images, _, columns, channels = x.shape
    block = images * columns
    first = pl.multiple_of(2 * info[0] * block, 64)
    taps = w.shape[0]

    def fill(k, carry):
        at = pl.multiple_of(k * columns, columns)
        down, up = shifted(mid[pl.ds(first + at, columns), :].astype(F32))
        side[0, pl.ds(at, columns), :] = down.astype(BF16)
        side[1, pl.ds(at, columns), :] = up.astype(BF16)
        return carry

    lax.fori_loop(0, 4 * images, fill, 0)
    rhs = w[...].reshape(taps * channels, channels)
    for r in range(2):
        lhs = []
        for t in range(taps):
            at = (r + t // 3) * block
            if t % 3 == 1:
                lhs.append(mid[pl.ds(pl.multiple_of(first + at, 64), block), :])
            else:
                lhs.append(side[(t % 3) // 2, at : at + block, :])
        value = jnp.dot(jnp.concatenate(lhs, axis=1), rhs, preferred_element_type=F32)
        value = value.reshape(images, columns, channels)
        out[:, r] = (x[:, r].astype(F32) + value).astype(BF16)


def back_kernel(info, places, *refs):
    pieces, refs = refs[:-17], refs[-17:]
    u, u_mate, rim_there, x, mean, rstd, gain, bias, out, sums, w = refs[:11]
    part, rim, one, two, sem, rim_sem = refs[11:]
    images, _, columns, channels = x.shape
    block = images * columns
    taps = w.shape[0]
    core = info[0]
    copies = [
        [
            pltpu.make_async_copy(
                piece.at[t],
                w.at[t, pl.ds(pl.multiple_of(places[k], 32), piece.shape[1]), :],
                sem.at[t, k],
            )
            for k, piece in enumerate(pieces)
        ]
        for t in range(taps)
    ]
    rim_copy = pltpu.make_async_copy(rim_there, rim, rim_sem)
    rim_copy.start()
    for tap in copies[:4]:
        for c in tap:
            c.start()

    def fill(load, row):
        def step(img, carry):
            value = load(img)
            down, up = shifted(value.astype(F32))
            at = pl.ds(pl.multiple_of((row * images + img) * columns, columns), columns)
            part[0, at, :] = down.astype(BF16)
            part[1, at, :] = value
            part[2, at, :] = up.astype(BF16)
            return carry

        lax.fori_loop(0, images, step, 0)

    fill(lambda img: u[img, 0], 1)
    fill(lambda img: u[img, 1], 2)
    fill(lambda img: u_mate[img, core], 3 - 3 * core)
    rim_copy.wait()
    for tap in copies[4:]:
        for c in tap:
            c.start()
    fill(lambda img: rim[img], 3 * core)

    for group in (range(0, 4), range(4, taps)):
        for t in group:
            for c in copies[t]:
                c.wait()
        rhs = jnp.concatenate([w[t] for t in group], axis=1)
        for r in range(2):
            lhs = jnp.concatenate([
                part[2 - t % 3, (r + 2 - t // 3) * block : (r + 3 - t // 3) * block, :]
                for t in group
            ], axis=1)
            value = lax.dot_general(
                lhs, rhs, (((1,), (1,)), ((), ())), preferred_element_type=F32
            ).reshape(images, columns, channels)
            if group[0] == 0:
                out[:, r] = value
            else:
                out[:, r] += value

    def finish(img, carry):
        first = jnp.zeros((1, channels), F32)
        second = jnp.zeros((1, channels), F32)
        for r in range(2):
            centred = (x[img, r].astype(F32) - mean[pl.ds(img, 1), :]) * rstd[pl.ds(img, 1), :]
            normed = centred * gain[...] + bias[...]
            s = 1.0 / (1.0 + jnp.exp(-normed))
            grad = out[img, r] * s * (1.0 + normed * (1.0 - s))
            out[img, r] = grad
            first = first + jnp.sum(grad, axis=0, keepdims=True)
            second = second + jnp.sum(grad * centred, axis=0, keepdims=True)
        one[pl.ds(img, 1), :] = first
        two[pl.ds(img, 1), :] = second
        return carry

    lax.fori_loop(0, images, finish, 0)
    groups = channels // GSIZE
    member = members(channels, groups)
    sums[...] = jnp.zeros_like(sums)
    sums[0:images, 0:groups] = to_groups(one[...] * gain[...], member)
    sums[0:images, groups : 2 * groups] = to_groups(two[...] * gain[...], member)
    base = images + images % 2
    rows = channels // LANES
    gain_part = jnp.sum(two[...], axis=0, keepdims=True)
    bias_part = jnp.sum(one[...], axis=0, keepdims=True)
    for k in range(rows):
        at = slice(k * LANES, (k + 1) * LANES)
        sums[base + k : base + k + 1, :] = gain_part[:, at]
        sums[base + rows + k : base + rows + k + 1, :] = bias_part[:, at]


def input_kernel(size, sums, grad, x, u, mean, rstd, gain, out):
    images, rows, columns, channels = x.shape
    groups = channels // GSIZE
    member = members(channels, groups)
    means = sums[...] / size
    first = to_chans(means[:images, :groups], member)
    second = to_chans(means[:images, groups : 2 * groups], member)
    for img in range(images):
        at = slice(img, img + 1)
        for r in range(rows):
            centred = (x[img, r].astype(F32) - mean[at]) * rstd[at]
            inner = grad[img, r] * gain[...] - first[at] - centred * second[at]
            out[img, r] = (u[img, r].astype(F32) + rstd[at] * inner).astype(BF16)


def body(inputs, norm_gain, norm_bias, conv_weight, upstream):
    images, rows, columns, channels = inputs.shape
    count, dps = lax.axis_size("space"), lax.axis_size("dp")
    me, half = lax.axis_index("space"), lax.axis_index("dp")
    core, mate = me & 1, me ^ 1
    groups = channels // GSIZE
    bits = count.bit_length() - 1
    size = float(rows * columns * GSIZE * count)
    block = images * columns
    two = dps == 2
    gain_row, bias_row = norm_gain[None], norm_bias[None]
    taps = conv_weight.shape[0]
    own_ok = jnp.where((me == 0) | (me == count - 1), 0, 1)
    mate_ok = jnp.where((mate == 0) | (mate == count - 1), 0, 1)
    info = jnp.stack(
        [core, own_ok, mate_ok, half if two else 0 * core, me]
    ).astype(jnp.int32)

    pairs = []
    for i in range(1, count - 1, 2):
        pairs += [(i, i + 1), (i + 1, i)]
    x_mate = swap(inputs, "space", 1)
    u_mate = swap(upstream, "space", 1)

    part = conv_weight.shape[1] // 2
    row_shape = (images, columns, channels)
    out_shape = [struct((2 * images, groups), F32), struct(row_shape, BF16), struct(row_shape, BF16)]
    operands = [info, inputs, in_hbm(upstream)]
    if two:
        out_shape.append(struct((taps, part, channels), BF16))
        operands.append(in_hbm(conv_weight))
    stats, edge_x, edge_u, *w_sent = kernel_call(
        stats_kernel, 16, tuple(out_shape), [S, V, H] + [H] * (len(operands) - 3), "stats",
        [pltpu.SemaphoreType.DMA((3,))],
    )(*operands)
    if two:
        w_low = swap(w_sent[0], "dp", 1)
    rim_x = lax.ppermute(edge_x, "space", pairs)
    lhs = kernel_call(
        functools.partial(turn_kernel, bits), 16, struct((channels // 2, 4 * block), BF16),
        [S, V, V], "turn", [pltpu.VMEM((4 * block, channels), BF16)],
    )(info, upstream, u_mate)
    for place in [0] + list(range(2, bits)) + [1]:
        if place == 1:
            stats, rim_x = lax.optimization_barrier((stats, rim_x))
        step = swap(stats, "space", 1 << place)
        if place == 2:
            step, lhs = lax.optimization_barrier((step, lhs))
        stats = stats + step
    rim_x_mate = swap(rim_x, "space", 1)
    rim_u = lax.ppermute(after(edge_u, stats), "space", pairs)

    act_mid, act_side, mean, rstd = kernel_call(
        functools.partial(act_kernel, size), 24,
        (
            struct((6 * block, channels), BF16),
            struct((2, 6 * block, channels), BF16),
            struct((images, channels), F32),
            struct((images, channels), F32),
        ),
        [S] + [V] * 7, "activate",
    )(info, stats, inputs, x_mate, rim_x, rim_x_mate, gain_row, bias_row)

    def fold(kept, got):
        shape = (kept.shape[0] // 2, kept.shape[1])
        return kernel_call(
            fold_kernel, 8, (struct(shape, BF16), struct(shape, F32)), [V, V], "fold"
        )(kept, got)

    def split(kept, got):
        shape = (kept.shape[0], kept.shape[1] // 2)
        return kernel_call(
            functools.partial(part_kernel, channels // 2), 8,
            (struct(shape, BF16), struct(shape, F32)), [S, V, V], "split",
        )(info, kept, got)

    width_a, width_b = len(GROUP_A) * channels, len(GROUP_B) * channels
    shape_b = (channels // 2, width_b // 2) if two else (channels // 4, width_b)
    shapes = [((channels // 4, width_a), BF16), ((channels // 4, width_a), F32)]
    shapes += [(shape_b, BF16), (shape_b, F32)]
    sent_a, kept_a, sent_b, kept_b = kernel_call(
        functools.partial(grad_kernel, block, two), 28,
        tuple(pltpu.HBM(*shape) for shape in shapes), [S] + [V] * 3, "weight_terms",
        [pltpu.VMEM(*shape) for shape in shapes] + [pltpu.SemaphoreType.DMA((10,))], (H,) * 4,
    )(info, lhs, act_mid, act_side)
    sent_a, sent_b, rim_u = lax.optimization_barrier((sent_a, sent_b, rim_u))
    got_a = swap(sent_a, "space", 4)
    got_b = swap(sent_b, "dp", 1) if two else swap(sent_b, "space", 4)

    if two:
        w_low = after(w_low, sent_b)
        other = (1 - half) * 2 * part
        spots = jnp.stack([half * 2 * part, other + core * part, other + (1 - core) * part])
        w_parts = [conv_weight, w_low, swap(w_low, "space", 1)]
    else:
        spots = jnp.zeros((1,), jnp.int32)
        w_parts = [lax.all_gather(conv_weight, "dp", axis=1, tiled=True)]
    grad, sums, weights = kernel_call(
        back_kernel, 32,
        (
            struct(inputs.shape, F32),
            struct((40, LANES), F32),
            struct((taps, channels, channels), BF16),
        ),
        [S, S] + [H] * len(w_parts) + [V, V, H] + [V] * 5, "conv_backward",
        [
            pltpu.VMEM((3, 4 * block, channels), BF16),
            pltpu.VMEM(row_shape, BF16),
            pltpu.VMEM((images, channels), F32),
            pltpu.VMEM((images, channels), F32),
            pltpu.SemaphoreType.DMA((taps, len(w_parts))),
            pltpu.SemaphoreType.DMA,
        ],
    )(
        after(info, sent_b), spots.astype(jnp.int32), *[in_hbm(value) for value in w_parts],
        upstream, u_mate, in_hbm(rim_u), inputs, mean, rstd, gain_row, bias_row,
    )

    base = images + images % 2
    last = base + 2 * channels // LANES
    for place in range(2):
        sums = sums + swap(sums, "space", 1 << place)
    totals = sums[base:last]
    if two:
        more = swap(totals, "dp", 1)
        sent_a, kept_a = split(kept_a, after(got_a, sums))
        got_a = swap(sent_a, "dp", 1)
        sent_b, kept_b = fold(kept_b, after(got_b, sent_a))
        got_b = swap(sent_b, "space", 2)
        totals = totals + after(more, sent_b)
    else:
        totals = lax.psum(totals, "dp")
    sums = jnp.concatenate([sums[:base], totals, sums[last:]])
    for place in range(2, bits):
        sums = sums + swap(sums, "space", 1 << place)
    sent_a, kept_a = fold(kept_a, after(got_a, sums))
    got_a = swap(sent_a, "space", 2)
    sent_b, kept_b = fold(kept_b, after(got_b, sent_a))
    got_b = swap(sent_b, "space", 4 if two else 2)
    sums = after(sums, sent_b)
    input_grad = kernel_call(
        functools.partial(input_kernel, size), 16, struct(inputs.shape, BF16), [V] * 7, "input_grad"
    )(sums, grad, inputs, upstream, mean, rstd, gain_row)
    totals = sums[base:last].reshape(2, channels)
    sent_a, kept_a = fold(kept_a, after(got_a, input_grad))
    got_a = swap(sent_a, "space", 8)
    sent_b, kept_b = fold(kept_b, after(got_b, sent_a))
    got_b = swap(sent_b, "space", 8)
    mixed = kernel_call(
        conv_kernel, 32, struct(inputs.shape, BF16), [S] + [V] * 3, "conv_forward",
        [pltpu.VMEM((2, 4 * block, channels), BF16)],
    )(after(info, sent_b), act_mid, weights, inputs)
    got_a = after(got_a, mixed)
    wide = channels // 2 if two else channels
    weight_grad = kernel_call(
        last_kernel, 16, struct((taps, kept_a.shape[0], wide), F32), [V] * 4, "last"
    )(kept_a, got_a, kept_b, got_b)
    if not two:
        weight_grad = lax.psum_scatter(weight_grad, "dp", scatter_dimension=2, tiled=True)
    weight_grad = weight_grad.transpose(0, 2, 1)
    return (mixed, input_grad, weight_grad, totals[0], totals[1])


def solution(mesh):
    in_specs = (
        P("dp", "space", None, None),
        P(),
        P(),
        P(None, "dp", None),
        P("dp", "space", None, None),
    )
    out_specs = (
        P("dp", "space", None, None),
        P("dp", "space", None, None),
        P(None, "dp", "space"),
        P(),
        P(),
    )
    return jax.shard_map(body, mesh=mesh, in_specs=in_specs, out_specs=out_specs, check_vma=False)
```

```python
import functools

import jax
import jax.numpy as jnp
from jax import lax
from jax.experimental import pallas as pl
from jax.experimental.pallas import tpu as pltpu
from jax.sharding import PartitionSpec as P

GSIZE = 40
EPS = 1e-05
GROUP_A, GROUP_B = (0, 1, 2, 3, 4), (5, 6, 7, 8)
LANES = 128
F32 = jnp.float32
BF16 = jnp.bfloat16
HIGHEST = lax.Precision.HIGHEST
VMEM_SPEC = pl.BlockSpec(memory_space=pltpu.VMEM)
SMEM_SPEC = pl.BlockSpec(memory_space=pltpu.SMEM)
HBM_SPEC = pl.BlockSpec(memory_space=pltpu.HBM)
MIB = 1 << 20
V, S, H = VMEM_SPEC, SMEM_SPEC, HBM_SPEC


def kernel_call(body, mib, out_shape, in_specs, name, scratch=(), out_specs=None):
    return pl.pallas_call(
        body,
        out_shape=out_shape,
        in_specs=in_specs,
        out_specs=out_specs or jax.tree.map(lambda _: VMEM_SPEC, out_shape),
        scratch_shapes=scratch,
        compiler_params=pltpu.CompilerParams(vmem_limit_bytes=mib * MIB),
        name=name,
    )


def struct(shape, dtype):
    return jax.ShapeDtypeStruct(shape, dtype)


def swap(value, axis, bit):
    count = lax.axis_size(axis)
    return lax.ppermute(value, axis, [(i, i ^ bit) for i in range(count)])


def in_hbm(value):
    return pltpu.with_memory_space_constraint(value, pltpu.HBM)


def after(value, *others):
    return lax.optimization_barrier((value,) + others)[0]


def members(channels, groups):
    chan = lax.broadcasted_iota(jnp.int32, (groups, channels), 1)
    first = lax.broadcasted_iota(jnp.int32, (groups, channels), 0) * GSIZE
    return ((chan >= first) & (chan < first + GSIZE)).astype(F32)


def to_groups(sums, member):
    return lax.dot_general(
        sums, member, (((1,), (1,)), ((), ())), precision=HIGHEST, preferred_element_type=F32
    )


def to_chans(values, member):
    return jnp.dot(values, member, precision=HIGHEST, preferred_element_type=F32)


def shifted(block):
    columns = block.shape[0]
    col = lax.broadcasted_iota(jnp.int32, block.shape, 0)
    down = jnp.where(col == 0, 0.0, pltpu.roll(block, 1, axis=0))
    up = jnp.where(col == columns - 1, 0.0, pltpu.roll(block, columns - 1, axis=0))
    return down, up


def slice_kernel(info, w, out, sem):
    rows = out.shape[1]
    at = pl.ds(pl.multiple_of(info[0] * rows, 32), rows)
    copy = pltpu.make_async_copy(w.at[:, at, :], out, sem)
    copy.start()
    copy.wait()


def stats_kernel(info, x, u, out, edge_x, edge_u, sem):
    images, _, _, channels = x.shape
    core = info[0]
    copies = [
        pltpu.make_async_copy(x.at[:, core], edge_x, sem.at[0]),
        pltpu.make_async_copy(u.at[:, core], edge_u, sem.at[1]),
    ]
    for c in copies:
        c.start()
    one, two = [], []
    for img in range(images):
        value = x[img].astype(F32).reshape(-1, channels)
        one.append(jnp.sum(value, axis=0, keepdims=True))
        two.append(jnp.sum(value * value, axis=0, keepdims=True))
    out[...] = to_groups(jnp.concatenate(one + two), members(channels, channels // GSIZE))
    for c in copies:
        c.wait()


def act_kernel(size, info, stats, x, x_mate, rim, rim_mate, gain, bias, mid, side, mean, rstd):
    images, _, columns, channels = x.shape
    core, own_ok, mate_ok = info[0], info[1], info[2]
    member = members(channels, channels // GSIZE)
    group_mean = stats[:images] / size
    group_rstd = lax.rsqrt(stats[images:] / size - group_mean * group_mean + EPS)
    mean[...] = to_chans(group_mean, member)
    rstd[...] = to_chans(group_rstd, member)

    def fill(load, row, keep):
        def step(img, carry):
            value = load(img).astype(F32)
            scale = rstd[pl.ds(img, 1), :] * gain[...]
            normed = (value - mean[pl.ds(img, 1), :]) * scale + bias[...]
            act = normed / (1.0 + jnp.exp(-normed))
            if keep is not None:
                act = jnp.where(keep > 0, act, 0.0)
            down, up = shifted(act)
            at = pl.ds(pl.multiple_of((row * images + img) * columns, columns), columns)
            mid[at, :] = act.astype(BF16)
            side[0, at, :] = down.astype(BF16)
            side[1, at, :] = up.astype(BF16)
            return carry

        lax.fori_loop(0, images, step, 0)

    fill(lambda img: x[img, 0], 1 + 2 * core, None)
    fill(lambda img: x[img, 1], 2 + 2 * core, None)
    fill(lambda img: x_mate[img, 0], 3 - 2 * core, None)
    fill(lambda img: x_mate[img, 1], 4 - 2 * core, None)
    fill(lambda img: rim[img], 5 * core, own_ok)
    fill(lambda img: rim_mate[img], 5 - 5 * core, mate_ok)


def turn_kernel(bits, info, u, u_mate, out, rows):
    images, _, columns, channels = u.shape
    core, me = info[0], info[4]
    block = images * columns
    for r in range(2):
        at = pl.multiple_of((r + 2 * core) * block, 64)
        rows[pl.ds(at, block), :] = u[:, r].reshape(block, channels)
        at = pl.multiple_of((r + 2 - 2 * core) * block, 64)
        rows[pl.ds(at, block), :] = u_mate[:, r].reshape(block, channels)
    width = channels >> bits
    row = lax.broadcasted_iota(jnp.int32, out.shape[:1] + (channels,), 0)
    chan = core * width + row
    for place in range(bits - 1):
        low = width << (bits - 2 - place)
        own = (me >> (place + 1)) & 1
        late = lax.rem(row, 2 * low) >= low
        chan = chan - jnp.where(late, low, 0)
        bit = jnp.where(late, own, 1 - own)
        chan = chan + bit * (width << (place + 1))
    index = lax.broadcasted_iota(jnp.int32, chan.shape, 1)
    table = (index == chan).astype(F32).astype(BF16)
    out[...] = lax.dot_general(
        table, rows[...], (((1,), (1,)), ((), ())), preferred_element_type=F32
    ).astype(BF16)


def tap_block(mid, side, t, start, rows):
    at = pl.ds(start, rows)
    return mid[at, :] if t % 3 == 1 else side[(t % 3) // 2, at, :]


def halves(value, part):
    taps = value.shape[1] // (2 * part)
    low = [value[:, 2 * t * part : (2 * t + 1) * part] for t in range(taps)]
    high = [value[:, (2 * t + 1) * part : (2 * t + 2) * part] for t in range(taps)]
    return jnp.concatenate(low, axis=1), jnp.concatenate(high, axis=1)


def second_bit(value):
    quarter = value.shape[0] // 4
    one, two, three, four = [value[k * quarter : (k + 1) * quarter] for k in range(4)]
    return jnp.concatenate([one, three]), jnp.concatenate([two, four])


def grad_kernel(block, by_dp, info, lhs, mid, side, *refs):
    outs, stages, sem = refs[:4], refs[4:8], refs[8]
    channels = mid.shape[1]
    copies = []
    for group, cut, base in ((GROUP_A, False, 0), (GROUP_B, by_dp, 2)):
        for first in range(0, len(group), 2):
            pair = group[first : first + 2]
            rhs = [tap_block(mid, side, t, (t // 3) * block, lhs.shape[1]) for t in pair]
            rhs = rhs[0] if len(rhs) == 1 else jnp.concatenate(rhs, axis=1)
            got = jnp.dot(lhs[...], rhs, preferred_element_type=F32)
            if cut:
                low, high = halves(got, channels // 2)
                sent = jnp.where(info[3] == 0, high, low)
                kept = jnp.where(info[3] == 0, low, high)
                start = first * channels // 2
            else:
                sent, kept = second_bit(got)
                start = first * channels
            at = slice(start, start + sent.shape[1])
            stages[base][:, at] = sent.astype(BF16)
            stages[base + 1][:, at] = kept
            for k in (base, base + 1):
                copy = pltpu.make_async_copy(
                    stages[k].at[:, at], outs[k].at[:, at], sem.at[len(copies)]
                )
                copy.start()
                copies.append(copy)
    for copy in copies:
        copy.wait()


def fold_kernel(kept, got, sent_out, kept_out):
    cut = sent_out.shape[0]
    sent_out[...] = (kept[:cut] + got[:cut].astype(F32)).astype(BF16)
    kept_out[...] = kept[cut:] + got[cut:].astype(F32)


def part_kernel(part, info, kept, got, sent_out, kept_out):
    low, high = halves(kept[...] + got[...].astype(F32), part)
    sent_out[...] = jnp.where(info[3] == 0, high, low).astype(BF16)
    kept_out[...] = jnp.where(info[3] == 0, low, high)


def last_kernel(kept_a, got_a, kept_b, got_b, out):
    part = out.shape[2]
    first = 0
    for kept, got in ((kept_a, got_a), (kept_b, got_b)):
        value = kept[...] + got[...].astype(F32)
        count = value.shape[1] // part
        for t in range(count):
            out[first + t] = value[:, t * part : (t + 1) * part]
        first += count


def own_kernel(columns, info, mid, out):
    def fill(k, carry):
        at = pl.ds(pl.multiple_of(k * columns, columns), columns)
        first = pl.multiple_of(2 * info[0] * (out.shape[1] // 4), 64)
        value = mid[pl.ds(first + pl.multiple_of(k * columns, columns), columns), :]
        down, up = shifted(value.astype(F32))
        out[0, at, :] = down.astype(BF16)
        out[1, at, :] = value
        out[2, at, :] = up.astype(BF16)
        return carry

    lax.fori_loop(0, out.shape[1] // columns, fill, 0)


def conv_kernel(own, w, x, out):
    images, _, columns, channels = x.shape
    block = images * columns
    taps = w.shape[0]
    rhs = w[...].reshape(taps * channels, channels)
    for r in range(2):
        lhs = jnp.concatenate([
            own[t % 3, (r + t // 3) * block : (r + t // 3 + 1) * block, :] for t in range(taps)
        ], axis=1)
        value = jnp.dot(lhs, rhs, preferred_element_type=F32)
        value = value.reshape(images, columns, channels)
        out[:, r] = (x[:, r].astype(F32) + value).astype(BF16)


def back_kernel(info, places, *refs):
    pieces, refs = refs[:-17], refs[-17:]
    u, u_mate, rim_there, x, mean, rstd, gain, bias, out, sums, w = refs[:11]
    part, rim, one, two, sem, rim_sem = refs[11:]
    images, _, columns, channels = x.shape
    block = images * columns
    taps = w.shape[0]
    core = info[0]
    copies = [
        [
            pltpu.make_async_copy(
                piece.at[t],
                w.at[t, pl.ds(pl.multiple_of(places[k], 32), piece.shape[1]), :],
                sem.at[t, k],
            )
            for k, piece in enumerate(pieces)
        ]
        for t in range(taps)
    ]
    rim_copy = pltpu.make_async_copy(rim_there, rim, rim_sem)
    rim_copy.start()
    for tap in copies[:4]:
        for c in tap:
            c.start()

    def fill(load, row):
        def step(img, carry):
            value = load(img)
            down, up = shifted(value.astype(F32))
            at = pl.ds(pl.multiple_of((row * images + img) * columns, columns), columns)
            part[0, at, :] = down.astype(BF16)
            part[1, at, :] = value
            part[2, at, :] = up.astype(BF16)
            return carry

        lax.fori_loop(0, images, step, 0)

    fill(lambda img: u[img, 0], 1)
    fill(lambda img: u[img, 1], 2)
    fill(lambda img: u_mate[img, core], 3 - 3 * core)
    rim_copy.wait()
    for tap in copies[4:]:
        for c in tap:
            c.start()
    fill(lambda img: rim[img], 3 * core)

    for group in (range(0, 4), range(4, taps)):
        for t in group:
            for c in copies[t]:
                c.wait()
        rhs = jnp.concatenate([w[t] for t in group], axis=1)
        for r in range(2):
            lhs = jnp.concatenate([
                part[2 - t % 3, (r + 2 - t // 3) * block : (r + 3 - t // 3) * block, :]
                for t in group
            ], axis=1)
            value = lax.dot_general(
                lhs, rhs, (((1,), (1,)), ((), ())), preferred_element_type=F32
            ).reshape(images, columns, channels)
            if group[0] == 0:
                out[:, r] = value
            else:
                out[:, r] += value

    def finish(img, carry):
        first = jnp.zeros((1, channels), F32)
        second = jnp.zeros((1, channels), F32)
        for r in range(2):
            centred = (x[img, r].astype(F32) - mean[pl.ds(img, 1), :]) * rstd[pl.ds(img, 1), :]
            normed = centred * gain[...] + bias[...]
            s = 1.0 / (1.0 + jnp.exp(-normed))
            grad = out[img, r] * s * (1.0 + normed * (1.0 - s))
            out[img, r] = grad
            first = first + jnp.sum(grad, axis=0, keepdims=True)
            second = second + jnp.sum(grad * centred, axis=0, keepdims=True)
        one[pl.ds(img, 1), :] = first
        two[pl.ds(img, 1), :] = second
        return carry

    lax.fori_loop(0, images, finish, 0)
    groups = channels // GSIZE
    member = members(channels, groups)
    sums[...] = jnp.zeros_like(sums)
    sums[0:images, 0:groups] = to_groups(one[...] * gain[...], member)
    sums[0:images, groups : 2 * groups] = to_groups(two[...] * gain[...], member)
    base = images + images % 2
    rows = channels // LANES
    gain_part = jnp.sum(two[...], axis=0, keepdims=True)
    bias_part = jnp.sum(one[...], axis=0, keepdims=True)
    for k in range(rows):
        at = slice(k * LANES, (k + 1) * LANES)
        sums[base + k : base + k + 1, :] = gain_part[:, at]
        sums[base + rows + k : base + rows + k + 1, :] = bias_part[:, at]


def input_kernel(size, sums, grad, x, u, mean, rstd, gain, out):
    images, rows, columns, channels = x.shape
    groups = channels // GSIZE
    member = members(channels, groups)
    means = sums[...] / size
    first = to_chans(means[:images, :groups], member)
    second = to_chans(means[:images, groups : 2 * groups], member)
    for img in range(images):
        at = slice(img, img + 1)
        for r in range(rows):
            centred = (x[img, r].astype(F32) - mean[at]) * rstd[at]
            inner = grad[img, r] * gain[...] - first[at] - centred * second[at]
            out[img, r] = (u[img, r].astype(F32) + rstd[at] * inner).astype(BF16)


def body(inputs, norm_gain, norm_bias, conv_weight, upstream):
    images, rows, columns, channels = inputs.shape
    count, dps = lax.axis_size("space"), lax.axis_size("dp")
    me, half = lax.axis_index("space"), lax.axis_index("dp")
    core, mate = me & 1, me ^ 1
    groups = channels // GSIZE
    bits = count.bit_length() - 1
    size = float(rows * columns * GSIZE * count)
    block = images * columns
    two = dps == 2
    gain_row, bias_row = norm_gain[None], norm_bias[None]
    taps = conv_weight.shape[0]
    own_ok = jnp.where((me == 0) | (me == count - 1), 0, 1)
    mate_ok = jnp.where((mate == 0) | (mate == count - 1), 0, 1)
    info = jnp.stack(
        [core, own_ok, mate_ok, half if two else 0 * core, me]
    ).astype(jnp.int32)

    pairs = []
    for i in range(1, count - 1, 2):
        pairs += [(i, i + 1), (i + 1, i)]
    x_mate = swap(inputs, "space", 1)
    u_mate = swap(upstream, "space", 1)

    part = conv_weight.shape[1] // 2
    row_shape = (images, columns, channels)
    first_info = info
    if two:
        w_sent = kernel_call(
            slice_kernel, 8, struct((taps, part, channels), BF16), [S, H], "slice",
            [pltpu.SemaphoreType.DMA],
        )(info, in_hbm(conv_weight))
        w_low = swap(w_sent, "dp", 1)
        first_info = after(info, w_sent)
    stats, edge_x, edge_u = kernel_call(
        stats_kernel, 16,
        (struct((2 * images, groups), F32), struct(row_shape, BF16), struct(row_shape, BF16)),
        [S, V, H], "stats", [pltpu.SemaphoreType.DMA((2,))],
    )(first_info, inputs, in_hbm(upstream))
    rim_x = lax.ppermute(edge_x, "space", pairs)
    lhs = kernel_call(
        functools.partial(turn_kernel, bits), 16, struct((channels // 2, 4 * block), BF16),
        [S, V, V], "turn", [pltpu.VMEM((4 * block, channels), BF16)],
    )(info, upstream, u_mate)
    for place in [0] + list(range(2, bits)) + [1]:
        if place == 1:
            stats, rim_x = lax.optimization_barrier((stats, rim_x))
        step = swap(stats, "space", 1 << place)
        if place == 2:
            step, lhs = lax.optimization_barrier((step, lhs))
        stats = stats + step
    rim_x_mate = swap(rim_x, "space", 1)
    rim_u = lax.ppermute(after(edge_u, stats), "space", pairs)

    act_mid, act_side, mean, rstd = kernel_call(
        functools.partial(act_kernel, size), 24,
        (
            struct((6 * block, channels), BF16),
            struct((2, 6 * block, channels), BF16),
            struct((images, channels), F32),
            struct((images, channels), F32),
        ),
        [S] + [V] * 7, "activate",
    )(info, stats, inputs, x_mate, rim_x, rim_x_mate, gain_row, bias_row)

    def fold(kept, got):
        shape = (kept.shape[0] // 2, kept.shape[1])
        return kernel_call(
            fold_kernel, 8, (struct(shape, BF16), struct(shape, F32)), [V, V], "fold"
        )(kept, got)

    def split(kept, got):
        shape = (kept.shape[0], kept.shape[1] // 2)
        return kernel_call(
            functools.partial(part_kernel, channels // 2), 8,
            (struct(shape, BF16), struct(shape, F32)), [S, V, V], "split",
        )(info, kept, got)

    width_a, width_b = len(GROUP_A) * channels, len(GROUP_B) * channels
    shape_b = (channels // 2, width_b // 2) if two else (channels // 4, width_b)
    shapes = [((channels // 4, width_a), BF16), ((channels // 4, width_a), F32)]
    shapes += [(shape_b, BF16), (shape_b, F32)]
    sent_a, kept_a, sent_b, kept_b = kernel_call(
        functools.partial(grad_kernel, block, two), 28,
        tuple(pltpu.HBM(*shape) for shape in shapes), [S] + [V] * 3, "weight_terms",
        [pltpu.VMEM(*shape) for shape in shapes] + [pltpu.SemaphoreType.DMA((10,))], (H,) * 4,
    )(info, lhs, act_mid, act_side)
    sent_a, sent_b, rim_u = lax.optimization_barrier((sent_a, sent_b, rim_u))
    got_a = swap(sent_a, "space", 4)
    got_b = swap(sent_b, "dp", 1) if two else swap(sent_b, "space", 4)

    if two:
        w_low = after(w_low, sent_b)
        other = (1 - half) * 2 * part
        spots = jnp.stack([half * 2 * part, other + core * part, other + (1 - core) * part])
        w_parts = [conv_weight, w_low, swap(w_low, "space", 1)]
    else:
        spots = jnp.zeros((1,), jnp.int32)
        w_parts = [lax.all_gather(conv_weight, "dp", axis=1, tiled=True)]
    grad, sums, weights = kernel_call(
        back_kernel, 32,
        (
            struct(inputs.shape, F32),
            struct((40, LANES), F32),
            struct((taps, channels, channels), BF16),
        ),
        [S, S] + [H] * len(w_parts) + [V, V, H] + [V] * 5, "conv_backward",
        [
            pltpu.VMEM((3, 4 * block, channels), BF16),
            pltpu.VMEM(row_shape, BF16),
            pltpu.VMEM((images, channels), F32),
            pltpu.VMEM((images, channels), F32),
            pltpu.SemaphoreType.DMA((taps, len(w_parts))),
            pltpu.SemaphoreType.DMA,
        ],
    )(
        after(info, sent_b), spots.astype(jnp.int32), *[in_hbm(value) for value in w_parts],
        upstream, u_mate, in_hbm(rim_u), inputs, mean, rstd, gain_row, bias_row,
    )

    base = images + images % 2
    last = base + 2 * channels // LANES
    for place in range(2):
        sums = sums + swap(sums, "space", 1 << place)
    totals = sums[base:last]
    if two:
        more = swap(totals, "dp", 1)
        sent_a, kept_a = split(kept_a, after(got_a, sums))
        got_a = swap(sent_a, "dp", 1)
        sent_b, kept_b = fold(kept_b, after(got_b, sent_a))
        got_b = swap(sent_b, "space", 2)
        totals = totals + after(more, sent_b)
    else:
        totals = lax.psum(totals, "dp")
    sums = jnp.concatenate([sums[:base], totals, sums[last:]])
    own = kernel_call(
        functools.partial(own_kernel, columns), 16, struct((3, 4 * block, channels), BF16),
        [S, V], "own",
    )(after(info, sent_b), act_mid)
    for place in range(2, bits):
        step = swap(sums, "space", 1 << place)
        if place == 2:
            step, own = lax.optimization_barrier((step, own))
        sums = sums + step
    sent_a, kept_a = fold(kept_a, after(got_a, sums))
    got_a = swap(sent_a, "space", 2)
    sent_b, kept_b = fold(kept_b, after(got_b, sent_a))
    got_b = swap(sent_b, "space", 4 if two else 2)
    sums = after(sums, sent_b)
    input_grad = kernel_call(
        functools.partial(input_kernel, size), 16, struct(inputs.shape, BF16), [V] * 7, "input_grad"
    )(sums, grad, inputs, upstream, mean, rstd, gain_row)
    totals = sums[base:last].reshape(2, channels)
    sent_a, kept_a = fold(kept_a, after(got_a, input_grad))
    got_a = swap(sent_a, "space", 8)
    sent_b, kept_b = fold(kept_b, after(got_b, sent_a))
    got_b = swap(sent_b, "space", 8)
    mixed = kernel_call(
        conv_kernel, 32, struct(inputs.shape, BF16), [V] * 3, "conv_forward"
    )(after(own, sent_b), weights, inputs)
    got_a = after(got_a, mixed)
    wide = channels // 2 if two else channels
    weight_grad = kernel_call(
        last_kernel, 16, struct((taps, kept_a.shape[0], wide), F32), [V] * 4, "last"
    )(kept_a, got_a, kept_b, got_b)
    if not two:
        weight_grad = lax.psum_scatter(weight_grad, "dp", scatter_dimension=2, tiled=True)
    weight_grad = weight_grad.transpose(0, 2, 1)
    return (mixed, input_grad, weight_grad, totals[0], totals[1])


def solution(mesh):
    in_specs = (
        P("dp", "space", None, None),
        P(),
        P(),
        P(None, "dp", None),
        P("dp", "space", None, None),
    )
    out_specs = (
        P("dp", "space", None, None),
        P("dp", "space", None, None),
        P(None, "dp", "space"),
        P(),
        P(),
    )
    return jax.shard_map(body, mesh=mesh, in_specs=in_specs, out_specs=out_specs, check_vma=False)
```

```python
import functools

import jax
import jax.numpy as jnp
from jax import lax
from jax.experimental import pallas as pl
from jax.experimental.pallas import tpu as pltpu
from jax.sharding import PartitionSpec as P

GSIZE = 40
EPS = 1e-05
GROUP_A, GROUP_B = (0, 1, 2, 3), (4, 5, 6, 7, 8)
LANES = 128
F32 = jnp.float32
BF16 = jnp.bfloat16
HIGHEST = lax.Precision.HIGHEST
VMEM_SPEC = pl.BlockSpec(memory_space=pltpu.VMEM)
SMEM_SPEC = pl.BlockSpec(memory_space=pltpu.SMEM)
HBM_SPEC = pl.BlockSpec(memory_space=pltpu.HBM)
MIB = 1 << 20
V, S, H = VMEM_SPEC, SMEM_SPEC, HBM_SPEC


def kernel_call(body, mib, out_shape, in_specs, name, scratch=(), out_specs=None):
    return pl.pallas_call(
        body,
        out_shape=out_shape,
        in_specs=in_specs,
        out_specs=out_specs or jax.tree.map(lambda _: VMEM_SPEC, out_shape),
        scratch_shapes=scratch,
        compiler_params=pltpu.CompilerParams(vmem_limit_bytes=mib * MIB),
        name=name,
    )


def struct(shape, dtype):
    return jax.ShapeDtypeStruct(shape, dtype)


def swap(value, axis, bit):
    count = lax.axis_size(axis)
    return lax.ppermute(value, axis, [(i, i ^ bit) for i in range(count)])


def in_hbm(value):
    return pltpu.with_memory_space_constraint(value, pltpu.HBM)


def after(value, *others):
    return lax.optimization_barrier((value,) + others)[0]


def members(channels, groups):
    chan = lax.broadcasted_iota(jnp.int32, (groups, channels), 1)
    first = lax.broadcasted_iota(jnp.int32, (groups, channels), 0) * GSIZE
    return ((chan >= first) & (chan < first + GSIZE)).astype(F32)


def to_groups(sums, member):
    return lax.dot_general(
        sums, member, (((1,), (1,)), ((), ())), precision=HIGHEST, preferred_element_type=F32
    )


def to_chans(values, member):
    return jnp.dot(values, member, precision=HIGHEST, preferred_element_type=F32)


def shifted(block):
    columns = block.shape[0]
    col = lax.broadcasted_iota(jnp.int32, block.shape, 0)
    down = jnp.where(col == 0, 0.0, pltpu.roll(block, 1, axis=0))
    up = jnp.where(col == columns - 1, 0.0, pltpu.roll(block, columns - 1, axis=0))
    return down, up


def slice_kernel(info, w, out, sem):
    rows = out.shape[1]
    at = pl.ds(pl.multiple_of(info[0] * rows, 32), rows)
    copy = pltpu.make_async_copy(w.at[:, at, :], out, sem)
    copy.start()
    copy.wait()


def stats_kernel(info, x, u, out, edge_x, edge_u, sem):
    images, _, _, channels = x.shape
    core = info[0]
    copies = [
        pltpu.make_async_copy(x.at[:, core], edge_x, sem.at[0]),
        pltpu.make_async_copy(u.at[:, core], edge_u, sem.at[1]),
    ]
    for c in copies:
        c.start()
    one, two = [], []
    for img in range(images):
        value = x[img].astype(F32).reshape(-1, channels)
        one.append(jnp.sum(value, axis=0, keepdims=True))
        two.append(jnp.sum(value * value, axis=0, keepdims=True))
    out[...] = to_groups(jnp.concatenate(one + two), members(channels, channels // GSIZE))
    for c in copies:
        c.wait()


def act_kernel(size, info, stats, x, x_mate, rim, rim_mate, gain, bias, mid, side, mean, rstd):
    images, _, columns, channels = x.shape
    core, own_ok, mate_ok = info[0], info[1], info[2]
    member = members(channels, channels // GSIZE)
    group_mean = stats[:images] / size
    group_rstd = lax.rsqrt(stats[images:] / size - group_mean * group_mean + EPS)
    mean[...] = to_chans(group_mean, member)
    rstd[...] = to_chans(group_rstd, member)

    def fill(load, row, keep):
        def step(img, carry):
            value = load(img).astype(F32)
            scale = rstd[pl.ds(img, 1), :] * gain[...]
            normed = (value - mean[pl.ds(img, 1), :]) * scale + bias[...]
            act = normed / (1.0 + jnp.exp(-normed))
            if keep is not None:
                act = jnp.where(keep > 0, act, 0.0)
            down, up = shifted(act)
            at = pl.ds(pl.multiple_of((row * images + img) * columns, columns), columns)
            mid[at, :] = act.astype(BF16)
            side[0, at, :] = down.astype(BF16)
            side[1, at, :] = up.astype(BF16)
            return carry

        lax.fori_loop(0, images, step, 0)

    fill(lambda img: x[img, 0], 1 + 2 * core, None)
    fill(lambda img: x[img, 1], 2 + 2 * core, None)
    fill(lambda img: x_mate[img, 0], 3 - 2 * core, None)
    fill(lambda img: x_mate[img, 1], 4 - 2 * core, None)
    fill(lambda img: rim[img], 5 * core, own_ok)
    fill(lambda img: rim_mate[img], 5 - 5 * core, mate_ok)


def turn_kernel(bits, info, u, u_mate, out, rows):
    images, _, columns, channels = u.shape
    core, me = info[0], info[4]
    block = images * columns
    for r in range(2):
        at = pl.multiple_of((r + 2 * core) * block, 64)
        rows[pl.ds(at, block), :] = u[:, r].reshape(block, channels)
        at = pl.multiple_of((r + 2 - 2 * core) * block, 64)
        rows[pl.ds(at, block), :] = u_mate[:, r].reshape(block, channels)
    width = channels >> bits
    row = lax.broadcasted_iota(jnp.int32, out.shape[:1] + (channels,), 0)
    chan = core * width + row
    for place in range(bits - 1):
        low = width << (bits - 2 - place)
        own = (me >> (place + 1)) & 1
        late = lax.rem(row, 2 * low) >= low
        chan = chan - jnp.where(late, low, 0)
        bit = jnp.where(late, own, 1 - own)
        chan = chan + bit * (width << (place + 1))
    index = lax.broadcasted_iota(jnp.int32, chan.shape, 1)
    table = (index == chan).astype(F32).astype(BF16)
    out[...] = lax.dot_general(
        table, rows[...], (((1,), (1,)), ((), ())), preferred_element_type=F32
    ).astype(BF16)


def tap_block(mid, side, t, start, rows):
    at = pl.ds(start, rows)
    return mid[at, :] if t % 3 == 1 else side[(t % 3) // 2, at, :]


def halves(value, part):
    taps = value.shape[1] // (2 * part)
    low = [value[:, 2 * t * part : (2 * t + 1) * part] for t in range(taps)]
    high = [value[:, (2 * t + 1) * part : (2 * t + 2) * part] for t in range(taps)]
    return jnp.concatenate(low, axis=1), jnp.concatenate(high, axis=1)


def second_bit(value):
    quarter = value.shape[0] // 4
    one, two, three, four = [value[k * quarter : (k + 1) * quarter] for k in range(4)]
    return jnp.concatenate([one, three]), jnp.concatenate([two, four])


def grad_kernel(block, by_dp, info, lhs, mid, side, *refs):
    outs, stages, sem = refs[:4], refs[4:8], refs[8]
    channels = mid.shape[1]
    copies = []
    for group, cut, base in ((GROUP_A, False, 0), (GROUP_B, by_dp, 2)):
        for first in range(0, len(group), 2):
            pair = group[first : first + 2]
            rhs = [tap_block(mid, side, t, (t // 3) * block, lhs.shape[1]) for t in pair]
            rhs = rhs[0] if len(rhs) == 1 else jnp.concatenate(rhs, axis=1)
            got = jnp.dot(lhs[...], rhs, preferred_element_type=F32)
            if cut:
                low, high = halves(got, channels // 2)
                sent = jnp.where(info[3] == 0, high, low)
                kept = jnp.where(info[3] == 0, low, high)
                start = first * channels // 2
            else:
                sent, kept = second_bit(got)
                start = first * channels
            at = slice(start, start + sent.shape[1])
            stages[base][:, at] = sent.astype(BF16)
            stages[base + 1][:, at] = kept
            for k in (base, base + 1):
                copy = pltpu.make_async_copy(
                    stages[k].at[:, at], outs[k].at[:, at], sem.at[len(copies)]
                )
                copy.start()
                copies.append(copy)
    for copy in copies:
        copy.wait()


def fold_kernel(kept, got, sent_out, kept_out):
    cut = sent_out.shape[0]
    sent_out[...] = (kept[:cut] + got[:cut].astype(F32)).astype(BF16)
    kept_out[...] = kept[cut:] + got[cut:].astype(F32)


def part_kernel(part, info, kept, got, sent_out, kept_out):
    low, high = halves(kept[...] + got[...].astype(F32), part)
    sent_out[...] = jnp.where(info[3] == 0, high, low).astype(BF16)
    kept_out[...] = jnp.where(info[3] == 0, low, high)


def last_kernel(kept_a, got_a, kept_b, got_b, out):
    part = out.shape[2]
    first = 0
    for kept, got in ((kept_a, got_a), (kept_b, got_b)):
        value = kept[...] + got[...].astype(F32)
        count = value.shape[1] // part
        for t in range(count):
            out[first + t] = value[:, t * part : (t + 1) * part]
        first += count


def own_kernel(columns, info, mid, out):
    def fill(k, carry):
        at = pl.ds(pl.multiple_of(k * columns, columns), columns)
        first = pl.multiple_of(2 * info[0] * (out.shape[1] // 4), 64)
        value = mid[pl.ds(first + pl.multiple_of(k * columns, columns), columns), :]
        down, up = shifted(value.astype(F32))
        out[0, at, :] = down.astype(BF16)
        out[1, at, :] = value
        out[2, at, :] = up.astype(BF16)
        return carry

    lax.fori_loop(0, out.shape[1] // columns, fill, 0)


def conv_row(row, own, w, x):
    images, _, columns, channels = x.shape
    block = images * columns
    taps = w.shape[0]
    lhs = jnp.concatenate([
        own[t % 3, (row + t // 3) * block : (row + t // 3 + 1) * block, :] for t in range(taps)
    ], axis=1)
    value = jnp.dot(lhs, w[...].reshape(taps * channels, channels), preferred_element_type=F32)
    return (x[:, row].astype(F32) + value.reshape(images, columns, channels)).astype(BF16)


def conv_first_kernel(own, w, x, out):
    out[...] = conv_row(0, own, w, x)


def conv_kernel(own, w, x, first, out):
    out[:, 0] = first[...]
    out[:, 1] = conv_row(1, own, w, x)


def back_kernel(info, places, *refs):
    pieces, refs = refs[:-17], refs[-17:]
    u, u_mate, rim_there, x, mean, rstd, gain, bias, out, sums, w = refs[:11]
    part, rim, one, two, sem, rim_sem = refs[11:]
    images, _, columns, channels = x.shape
    block = images * columns
    taps = w.shape[0]
    core = info[0]
    copies = [
        [
            pltpu.make_async_copy(
                piece.at[t],
                w.at[t, pl.ds(pl.multiple_of(places[k], 32), piece.shape[1]), :],
                sem.at[t, k],
            )
            for k, piece in enumerate(pieces)
        ]
        for t in range(taps)
    ]
    rim_copy = pltpu.make_async_copy(rim_there, rim, rim_sem)
    rim_copy.start()
    for tap in copies[:4]:
        for c in tap:
            c.start()

    def fill(load, row):
        def step(img, carry):
            value = load(img)
            down, up = shifted(value.astype(F32))
            at = pl.ds(pl.multiple_of((row * images + img) * columns, columns), columns)
            part[0, at, :] = down.astype(BF16)
            part[1, at, :] = value
            part[2, at, :] = up.astype(BF16)
            return carry

        lax.fori_loop(0, images, step, 0)

    fill(lambda img: u[img, 0], 1)
    fill(lambda img: u[img, 1], 2)
    fill(lambda img: u_mate[img, core], 3 - 3 * core)
    rim_copy.wait()
    for tap in copies[4:]:
        for c in tap:
            c.start()
    fill(lambda img: rim[img], 3 * core)

    for group in (range(0, 4), range(4, taps)):
        for t in group:
            for c in copies[t]:
                c.wait()
        rhs = jnp.concatenate([w[t] for t in group], axis=1)
        for r in range(2):
            lhs = jnp.concatenate([
                part[2 - t % 3, (r + 2 - t // 3) * block : (r + 3 - t // 3) * block, :]
                for t in group
            ], axis=1)
            value = lax.dot_general(
                lhs, rhs, (((1,), (1,)), ((), ())), preferred_element_type=F32
            ).reshape(images, columns, channels)
            if group[0] == 0:
                out[:, r] = value
            else:
                out[:, r] += value

    def finish(img, carry):
        first = jnp.zeros((1, channels), F32)
        second = jnp.zeros((1, channels), F32)
        for r in range(2):
            centred = (x[img, r].astype(F32) - mean[pl.ds(img, 1), :]) * rstd[pl.ds(img, 1), :]
            normed = centred * gain[...] + bias[...]
            s = 1.0 / (1.0 + jnp.exp(-normed))
            grad = out[img, r] * s * (1.0 + normed * (1.0 - s))
            out[img, r] = grad
            first = first + jnp.sum(grad, axis=0, keepdims=True)
            second = second + jnp.sum(grad * centred, axis=0, keepdims=True)
        one[pl.ds(img, 1), :] = first
        two[pl.ds(img, 1), :] = second
        return carry

    lax.fori_loop(0, images, finish, 0)
    groups = channels // GSIZE
    member = members(channels, groups)
    sums[...] = jnp.zeros_like(sums)
    sums[0:images, 0:groups] = to_groups(one[...] * gain[...], member)
    sums[0:images, groups : 2 * groups] = to_groups(two[...] * gain[...], member)
    base = images + images % 2
    rows = channels // LANES
    gain_part = jnp.sum(two[...], axis=0, keepdims=True)
    bias_part = jnp.sum(one[...], axis=0, keepdims=True)
    for k in range(rows):
        at = slice(k * LANES, (k + 1) * LANES)
        sums[base + k : base + k + 1, :] = gain_part[:, at]
        sums[base + rows + k : base + rows + k + 1, :] = bias_part[:, at]


def input_kernel(size, sums, grad, x, u, mean, rstd, gain, out):
    images, rows, columns, channels = x.shape
    groups = channels // GSIZE
    member = members(channels, groups)
    means = sums[...] / size
    first = to_chans(means[:images, :groups], member)
    second = to_chans(means[:images, groups : 2 * groups], member)
    for img in range(images):
        at = slice(img, img + 1)
        for r in range(rows):
            centred = (x[img, r].astype(F32) - mean[at]) * rstd[at]
            inner = grad[img, r] * gain[...] - first[at] - centred * second[at]
            out[img, r] = (u[img, r].astype(F32) + rstd[at] * inner).astype(BF16)


def body(inputs, norm_gain, norm_bias, conv_weight, upstream):
    images, rows, columns, channels = inputs.shape
    count, dps = lax.axis_size("space"), lax.axis_size("dp")
    me, half = lax.axis_index("space"), lax.axis_index("dp")
    core, mate = me & 1, me ^ 1
    groups = channels // GSIZE
    bits = count.bit_length() - 1
    size = float(rows * columns * GSIZE * count)
    block = images * columns
    two = dps == 2
    gain_row, bias_row = norm_gain[None], norm_bias[None]
    taps = conv_weight.shape[0]
    own_ok = jnp.where((me == 0) | (me == count - 1), 0, 1)
    mate_ok = jnp.where((mate == 0) | (mate == count - 1), 0, 1)
    info = jnp.stack(
        [core, own_ok, mate_ok, half if two else 0 * core, me]
    ).astype(jnp.int32)

    pairs = []
    for i in range(1, count - 1, 2):
        pairs += [(i, i + 1), (i + 1, i)]
    x_mate = swap(inputs, "space", 1)
    u_mate = swap(upstream, "space", 1)

    part = conv_weight.shape[1] // 2
    row_shape = (images, columns, channels)
    first_info = info
    if two:
        w_sent = kernel_call(
            slice_kernel, 8, struct((taps, part, channels), BF16), [S, H], "slice",
            [pltpu.SemaphoreType.DMA],
        )(info, in_hbm(conv_weight))
        w_low = swap(w_sent, "dp", 1)
        first_info = after(info, w_sent)
    stats, edge_x, edge_u = kernel_call(
        stats_kernel, 16,
        (struct((2 * images, groups), F32), struct(row_shape, BF16), struct(row_shape, BF16)),
        [S, V, H], "stats", [pltpu.SemaphoreType.DMA((2,))],
    )(first_info, inputs, in_hbm(upstream))
    rim_x = lax.ppermute(edge_x, "space", pairs)
    lhs = kernel_call(
        functools.partial(turn_kernel, bits), 16, struct((channels // 2, 4 * block), BF16),
        [S, V, V], "turn", [pltpu.VMEM((4 * block, channels), BF16)],
    )(info, upstream, u_mate)
    for place in [0] + list(range(2, bits)) + [1]:
        if place == 1:
            stats, rim_x = lax.optimization_barrier((stats, rim_x))
        step = swap(stats, "space", 1 << place)
        if place == 2:
            step, lhs = lax.optimization_barrier((step, lhs))
        stats = stats + step
    rim_x_mate = swap(rim_x, "space", 1)
    rim_u = lax.ppermute(after(edge_u, stats), "space", pairs)

    act_mid, act_side, mean, rstd = kernel_call(
        functools.partial(act_kernel, size), 24,
        (
            struct((6 * block, channels), BF16),
            struct((2, 6 * block, channels), BF16),
            struct((images, channels), F32),
            struct((images, channels), F32),
        ),
        [S] + [V] * 7, "activate",
    )(info, stats, inputs, x_mate, rim_x, rim_x_mate, gain_row, bias_row)

    def fold(kept, got):
        shape = (kept.shape[0] // 2, kept.shape[1])
        return kernel_call(
            fold_kernel, 8, (struct(shape, BF16), struct(shape, F32)), [V, V], "fold"
        )(kept, got)

    def split(kept, got):
        shape = (kept.shape[0], kept.shape[1] // 2)
        return kernel_call(
            functools.partial(part_kernel, channels // 2), 8,
            (struct(shape, BF16), struct(shape, F32)), [S, V, V], "split",
        )(info, kept, got)

    width_a, width_b = len(GROUP_A) * channels, len(GROUP_B) * channels
    shape_b = (channels // 2, width_b // 2) if two else (channels // 4, width_b)
    shapes = [((channels // 4, width_a), BF16), ((channels // 4, width_a), F32)]
    shapes += [(shape_b, BF16), (shape_b, F32)]
    sent_a, kept_a, sent_b, kept_b = kernel_call(
        functools.partial(grad_kernel, block, two), 28,
        tuple(pltpu.HBM(*shape) for shape in shapes), [S] + [V] * 3, "weight_terms",
        [pltpu.VMEM(*shape) for shape in shapes] + [pltpu.SemaphoreType.DMA((10,))], (H,) * 4,
    )(info, lhs, act_mid, act_side)
    sent_a, sent_b, rim_u = lax.optimization_barrier((sent_a, sent_b, rim_u))
    got_a = swap(sent_a, "space", 4)
    got_b = swap(sent_b, "dp", 1) if two else swap(sent_b, "space", 4)

    if two:
        w_low = after(w_low, sent_b)
        other = (1 - half) * 2 * part
        spots = jnp.stack([half * 2 * part, other + core * part, other + (1 - core) * part])
        w_parts = [conv_weight, w_low, swap(w_low, "space", 1)]
    else:
        spots = jnp.zeros((1,), jnp.int32)
        w_parts = [lax.all_gather(conv_weight, "dp", axis=1, tiled=True)]
    grad, sums, weights = kernel_call(
        back_kernel, 32,
        (
            struct(inputs.shape, F32),
            struct((40, LANES), F32),
            struct((taps, channels, channels), BF16),
        ),
        [S, S] + [H] * len(w_parts) + [V, V, H] + [V] * 5, "conv_backward",
        [
            pltpu.VMEM((3, 4 * block, channels), BF16),
            pltpu.VMEM(row_shape, BF16),
            pltpu.VMEM((images, channels), F32),
            pltpu.VMEM((images, channels), F32),
            pltpu.SemaphoreType.DMA((taps, len(w_parts))),
            pltpu.SemaphoreType.DMA,
        ],
    )(
        after(info, sent_b), spots.astype(jnp.int32), *[in_hbm(value) for value in w_parts],
        upstream, u_mate, in_hbm(rim_u), inputs, mean, rstd, gain_row, bias_row,
    )

    base = images + images % 2
    last = base + 2 * channels // LANES
    for place in range(2):
        sums = sums + swap(sums, "space", 1 << place)
    if two:
        sent_a, kept_a = split(kept_a, after(got_a, sums))
        got_a = swap(sent_a, "dp", 1)
        sent_b, kept_b = fold(kept_b, after(got_b, sent_a))
        got_b = swap(sent_b, "space", 2)
    own = kernel_call(
        functools.partial(own_kernel, columns), 16, struct((3, 4 * block, channels), BF16),
        [S, V], "own",
    )(after(info, sent_b), act_mid)
    for place in range(2, bits):
        step = swap(sums, "space", 1 << place)
        if place == 2:
            step, own = lax.optimization_barrier((step, own))
        if place == 3:
            first_row = kernel_call(
                conv_first_kernel, 32, struct(row_shape, BF16), [V] * 3, "conv_forward"
            )(after(own, sums), weights, inputs)
            step, first_row = lax.optimization_barrier((step, first_row))
        sums = sums + step
    sent_a, kept_a = fold(kept_a, after(got_a, sums))
    got_a = swap(sent_a, "space", 2)
    sent_b, kept_b = fold(kept_b, after(got_b, sent_a))
    got_b = swap(sent_b, "space", 4 if two else 2)
    sums = after(sums, sent_b)
    input_grad = kernel_call(
        functools.partial(input_kernel, size), 16, struct(inputs.shape, BF16), [V] * 7, "input_grad"
    )(sums, grad, inputs, upstream, mean, rstd, gain_row)
    totals = sums[base:last]
    more = swap(totals, "dp", 1) if two else lax.psum(totals, "dp")
    sent_a, kept_a = fold(kept_a, after(got_a, input_grad))
    got_a = swap(sent_a, "space", 8)
    sent_b, kept_b = fold(kept_b, after(got_b, sent_a))
    got_b = swap(sent_b, "space", 8)
    mixed = kernel_call(
        conv_kernel, 32, struct(inputs.shape, BF16), [V] * 4, "conv_forward"
    )(after(own, sent_b), weights, inputs, first_row)
    got_a, more = lax.optimization_barrier((got_a, more, mixed))[:2]
    totals = (totals + more if two else more).reshape(2, channels)
    wide = channels // 2 if two else channels
    weight_grad = kernel_call(
        last_kernel, 16, struct((taps, kept_a.shape[0], wide), F32), [V] * 4, "last"
    )(kept_a, got_a, kept_b, got_b)
    if not two:
        weight_grad = lax.psum_scatter(weight_grad, "dp", scatter_dimension=2, tiled=True)
    weight_grad = weight_grad.transpose(0, 2, 1)
    return (mixed, input_grad, weight_grad, totals[0], totals[1])


def solution(mesh):
    in_specs = (
        P("dp", "space", None, None),
        P(),
        P(),
        P(None, "dp", None),
        P("dp", "space", None, None),
    )
    out_specs = (
        P("dp", "space", None, None),
        P("dp", "space", None, None),
        P(None, "dp", "space"),
        P(),
        P(),
    )
    return jax.shard_map(body, mesh=mesh, in_specs=in_specs, out_specs=out_specs, check_vma=False)
```

```python
import functools

import jax
import jax.numpy as jnp
from jax import lax
from jax.experimental import pallas as pl
from jax.experimental.pallas import tpu as pltpu
from jax.sharding import PartitionSpec as P

GSIZE = 40
EPS = 1e-05
GROUP_A, GROUP_B = (0, 1, 2, 3), (4, 5, 6, 7, 8)
LANES = 128
F32 = jnp.float32
BF16 = jnp.bfloat16
HIGHEST = lax.Precision.HIGHEST
VMEM_SPEC = pl.BlockSpec(memory_space=pltpu.VMEM)
SMEM_SPEC = pl.BlockSpec(memory_space=pltpu.SMEM)
HBM_SPEC = pl.BlockSpec(memory_space=pltpu.HBM)
MIB = 1 << 20
V, S, H = VMEM_SPEC, SMEM_SPEC, HBM_SPEC


def kernel_call(body, mib, out_shape, in_specs, name, scratch=(), out_specs=None):
    return pl.pallas_call(
        body,
        out_shape=out_shape,
        in_specs=in_specs,
        out_specs=out_specs or jax.tree.map(lambda _: VMEM_SPEC, out_shape),
        scratch_shapes=scratch,
        compiler_params=pltpu.CompilerParams(vmem_limit_bytes=mib * MIB),
        name=name,
    )


def struct(shape, dtype):
    return jax.ShapeDtypeStruct(shape, dtype)


def swap(value, axis, bit):
    count = lax.axis_size(axis)
    return lax.ppermute(value, axis, [(i, i ^ bit) for i in range(count)])


def in_hbm(value):
    return pltpu.with_memory_space_constraint(value, pltpu.HBM)


def after(value, *others):
    return lax.optimization_barrier((value,) + others)[0]


def members(channels, groups):
    chan = lax.broadcasted_iota(jnp.int32, (groups, channels), 1)
    first = lax.broadcasted_iota(jnp.int32, (groups, channels), 0) * GSIZE
    return ((chan >= first) & (chan < first + GSIZE)).astype(F32)


def to_groups(sums, member):
    return lax.dot_general(
        sums, member, (((1,), (1,)), ((), ())), precision=HIGHEST, preferred_element_type=F32
    )


def to_chans(values, member):
    return jnp.dot(values, member, precision=HIGHEST, preferred_element_type=F32)


def shifted(block):
    columns = block.shape[0]
    col = lax.broadcasted_iota(jnp.int32, block.shape, 0)
    down = jnp.where(col == 0, 0.0, pltpu.roll(block, 1, axis=0))
    up = jnp.where(col == columns - 1, 0.0, pltpu.roll(block, columns - 1, axis=0))
    return down, up


def slice_kernel(info, w, out, sem):
    rows = out.shape[1]
    at = pl.ds(pl.multiple_of(info[0] * rows, 32), rows)
    copy = pltpu.make_async_copy(w.at[:, at, :], out, sem)
    copy.start()
    copy.wait()


def stats_kernel(info, x, u, out, edge_x, edge_u, sem):
    images, _, _, channels = x.shape
    core = info[0]
    copies = [
        pltpu.make_async_copy(x.at[:, core], edge_x, sem.at[0]),
        pltpu.make_async_copy(u.at[:, core], edge_u, sem.at[1]),
    ]
    for c in copies:
        c.start()
    one, two = [], []
    for img in range(images):
        value = x[img].astype(F32).reshape(-1, channels)
        one.append(jnp.sum(value, axis=0, keepdims=True))
        two.append(jnp.sum(value * value, axis=0, keepdims=True))
    out[...] = to_groups(jnp.concatenate(one + two), members(channels, channels // GSIZE))
    for c in copies:
        c.wait()


def act_kernel(size, info, stats, x, x_mate, rim, rim_mate, gain, bias, mid, side, mean, rstd):
    images, _, columns, channels = x.shape
    core, own_ok, mate_ok = info[0], info[1], info[2]
    member = members(channels, channels // GSIZE)
    group_mean = stats[:images] / size
    group_rstd = lax.rsqrt(stats[images:] / size - group_mean * group_mean + EPS)
    mean[...] = to_chans(group_mean, member)
    rstd[...] = to_chans(group_rstd, member)

    def fill(load, row, keep):
        def step(img, carry):
            value = load(img).astype(F32)
            scale = rstd[pl.ds(img, 1), :] * gain[...]
            normed = (value - mean[pl.ds(img, 1), :]) * scale + bias[...]
            act = normed / (1.0 + jnp.exp(-normed))
            if keep is not None:
                act = jnp.where(keep > 0, act, 0.0)
            down, up = shifted(act)
            at = pl.ds(pl.multiple_of((row * images + img) * columns, columns), columns)
            mid[at, :] = act.astype(BF16)
            side[0, at, :] = down.astype(BF16)
            side[1, at, :] = up.astype(BF16)
            return carry

        lax.fori_loop(0, images, step, 0)

    fill(lambda img: x[img, 0], 1 + 2 * core, None)
    fill(lambda img: x[img, 1], 2 + 2 * core, None)
    fill(lambda img: x_mate[img, 0], 3 - 2 * core, None)
    fill(lambda img: x_mate[img, 1], 4 - 2 * core, None)
    fill(lambda img: rim[img], 5 * core, own_ok)
    fill(lambda img: rim_mate[img], 5 - 5 * core, mate_ok)


def turn_kernel(bits, info, u, u_mate, out, rows):
    images, _, columns, channels = u.shape
    core, me = info[0], info[4]
    block = images * columns
    for r in range(2):
        at = pl.multiple_of((r + 2 * core) * block, 64)
        rows[pl.ds(at, block), :] = u[:, r].reshape(block, channels)
        at = pl.multiple_of((r + 2 - 2 * core) * block, 64)
        rows[pl.ds(at, block), :] = u_mate[:, r].reshape(block, channels)
    width = channels >> bits
    row = lax.broadcasted_iota(jnp.int32, out.shape[:1] + (channels,), 0)
    chan = core * width + row
    for place in range(bits - 1):
        low = width << (bits - 2 - place)
        own = (me >> (place + 1)) & 1
        late = lax.rem(row, 2 * low) >= low
        chan = chan - jnp.where(late, low, 0)
        bit = jnp.where(late, own, 1 - own)
        chan = chan + bit * (width << (place + 1))
    index = lax.broadcasted_iota(jnp.int32, chan.shape, 1)
    table = (index == chan).astype(F32).astype(BF16)
    out[...] = lax.dot_general(
        table, rows[...], (((1,), (1,)), ((), ())), preferred_element_type=F32
    ).astype(BF16)


def tap_block(mid, side, t, start, rows):
    at = pl.ds(start, rows)
    return mid[at, :] if t % 3 == 1 else side[(t % 3) // 2, at, :]


def halves(value, part):
    taps = value.shape[1] // (2 * part)
    low = [value[:, 2 * t * part : (2 * t + 1) * part] for t in range(taps)]
    high = [value[:, (2 * t + 1) * part : (2 * t + 2) * part] for t in range(taps)]
    return jnp.concatenate(low, axis=1), jnp.concatenate(high, axis=1)


def second_bit(value):
    quarter = value.shape[0] // 4
    one, two, three, four = [value[k * quarter : (k + 1) * quarter] for k in range(4)]
    return jnp.concatenate([one, three]), jnp.concatenate([two, four])


def grad_kernel(block, by_dp, info, lhs, mid, side, *refs):
    outs, stages, sem = refs[:4], refs[4:8], refs[8]
    channels = mid.shape[1]
    copies = []
    for group, cut, base in ((GROUP_A, False, 0), (GROUP_B, by_dp, 2)):
        for first in range(0, len(group), 2):
            pair = group[first : first + 2]
            rhs = [tap_block(mid, side, t, (t // 3) * block, lhs.shape[1]) for t in pair]
            rhs = rhs[0] if len(rhs) == 1 else jnp.concatenate(rhs, axis=1)
            got = jnp.dot(lhs[...], rhs, preferred_element_type=F32)
            if cut:
                low, high = halves(got, channels // 2)
                sent = jnp.where(info[3] == 0, high, low)
                kept = jnp.where(info[3] == 0, low, high)
                start = first * channels // 2
            else:
                sent, kept = second_bit(got)
                start = first * channels
            at = slice(start, start + sent.shape[1])
            stages[base][:, at] = sent.astype(BF16)
            stages[base + 1][:, at] = kept
            for k in (base, base + 1):
                copy = pltpu.make_async_copy(
                    stages[k].at[:, at], outs[k].at[:, at], sem.at[len(copies)]
                )
                copy.start()
                copies.append(copy)
    for copy in copies:
        copy.wait()


def fold_kernel(kept, got, sent_out, kept_out):
    cut = sent_out.shape[0]
    sent_out[...] = (kept[:cut] + got[:cut].astype(F32)).astype(BF16)
    kept_out[...] = kept[cut:] + got[cut:].astype(F32)


def part_kernel(part, info, kept, got, sent_out, kept_out):
    low, high = halves(kept[...] + got[...].astype(F32), part)
    sent_out[...] = jnp.where(info[3] == 0, high, low).astype(BF16)
    kept_out[...] = jnp.where(info[3] == 0, low, high)


def last_kernel(kept_a, got_a, kept_b, got_b, out):
    part = out.shape[2]
    first = 0
    for kept, got in ((kept_a, got_a), (kept_b, got_b)):
        value = kept[...] + got[...].astype(F32)
        count = value.shape[1] // part
        for t in range(count):
            out[first + t] = value[:, t * part : (t + 1) * part]
        first += count


def own_kernel(columns, info, mid, out):
    def fill(k, carry):
        at = pl.ds(pl.multiple_of(k * columns, columns), columns)
        first = pl.multiple_of(2 * info[0] * (out.shape[1] // 4), 64)
        value = mid[pl.ds(first + pl.multiple_of(k * columns, columns), columns), :]
        down, up = shifted(value.astype(F32))
        out[0, at, :] = down.astype(BF16)
        out[1, at, :] = value
        out[2, at, :] = up.astype(BF16)
        return carry

    lax.fori_loop(0, out.shape[1] // columns, fill, 0)


def conv_row(row, own, w, x):
    images, _, columns, channels = x.shape
    block = images * columns
    taps = w.shape[0]
    lhs = jnp.concatenate([
        own[t % 3, (row + t // 3) * block : (row + t // 3 + 1) * block, :] for t in range(taps)
    ], axis=1)
    value = jnp.dot(lhs, w[...].reshape(taps * channels, channels), preferred_element_type=F32)
    return (x[:, row].astype(F32) + value.reshape(images, columns, channels)).astype(BF16)


def conv_first_kernel(own, w, x, out):
    out[...] = conv_row(0, own, w, x)


def conv_kernel(own, w, x, first, out):
    out[:, 0] = first[...]
    out[:, 1] = conv_row(1, own, w, x)


def back_kernel(info, places, *refs):
    pieces, refs = refs[:-17], refs[-17:]
    u, u_mate, rim_there, x, mean, rstd, gain, bias, out, sums, w = refs[:11]
    part, rim, one, two, sem, rim_sem = refs[11:]
    images, _, columns, channels = x.shape
    block = images * columns
    taps = w.shape[0]
    core = info[0]
    copies = [
        [
            pltpu.make_async_copy(
                piece.at[t],
                w.at[t, pl.ds(pl.multiple_of(places[k], 32), piece.shape[1]), :],
                sem.at[t, k],
            )
            for k, piece in enumerate(pieces)
        ]
        for t in range(taps)
    ]
    rim_copy = pltpu.make_async_copy(rim_there, rim, rim_sem)
    rim_copy.start()
    for tap in copies[:4]:
        for c in tap:
            c.start()

    def fill(load, row):
        def step(img, carry):
            value = load(img)
            down, up = shifted(value.astype(F32))
            at = pl.ds(pl.multiple_of((row * images + img) * columns, columns), columns)
            part[0, at, :] = down.astype(BF16)
            part[1, at, :] = value
            part[2, at, :] = up.astype(BF16)
            return carry

        lax.fori_loop(0, images, step, 0)

    fill(lambda img: u[img, 0], 1)
    fill(lambda img: u[img, 1], 2)
    fill(lambda img: u_mate[img, core], 3 - 3 * core)
    rim_copy.wait()
    for tap in copies[4:]:
        for c in tap:
            c.start()
    fill(lambda img: rim[img], 3 * core)

    for group in (range(0, 4), range(4, taps)):
        for t in group:
            for c in copies[t]:
                c.wait()
        rhs = jnp.concatenate([w[t] for t in group], axis=1)
        for r in range(2):
            lhs = jnp.concatenate([
                part[2 - t % 3, (r + 2 - t // 3) * block : (r + 3 - t // 3) * block, :]
                for t in group
            ], axis=1)
            value = lax.dot_general(
                lhs, rhs, (((1,), (1,)), ((), ())), preferred_element_type=F32
            ).reshape(images, columns, channels)
            if group[0] == 0:
                out[:, r] = value
            else:
                out[:, r] += value

    def finish(img, carry):
        first = jnp.zeros((1, channels), F32)
        second = jnp.zeros((1, channels), F32)
        for r in range(2):
            centred = (x[img, r].astype(F32) - mean[pl.ds(img, 1), :]) * rstd[pl.ds(img, 1), :]
            normed = centred * gain[...] + bias[...]
            s = 0.5 + 0.5 * jnp.tanh(0.5 * normed)
            grad = out[img, r] * s * (1.0 + normed * (1.0 - s))
            out[img, r] = grad
            first = first + jnp.sum(grad, axis=0, keepdims=True)
            second = second + jnp.sum(grad * centred, axis=0, keepdims=True)
        one[pl.ds(img, 1), :] = first
        two[pl.ds(img, 1), :] = second
        return carry

    lax.fori_loop(0, images, finish, 0)
    groups = channels // GSIZE
    member = members(channels, groups)
    sums[...] = jnp.zeros_like(sums)
    sums[0:images, 0:groups] = to_groups(one[...] * gain[...], member)
    sums[0:images, groups : 2 * groups] = to_groups(two[...] * gain[...], member)
    base = images + images % 2
    rows = channels // LANES
    gain_part = jnp.sum(two[...], axis=0, keepdims=True)
    bias_part = jnp.sum(one[...], axis=0, keepdims=True)
    for k in range(rows):
        at = slice(k * LANES, (k + 1) * LANES)
        sums[base + k : base + k + 1, :] = gain_part[:, at]
        sums[base + rows + k : base + rows + k + 1, :] = bias_part[:, at]


def input_kernel(size, sums, grad, x, u, mean, rstd, gain, out):
    images, rows, columns, channels = x.shape
    groups = channels // GSIZE
    member = members(channels, groups)
    means = sums[...] / size
    first = to_chans(means[:images, :groups], member)
    second = to_chans(means[:images, groups : 2 * groups], member)
    for img in range(images):
        at = slice(img, img + 1)
        for r in range(rows):
            centred = (x[img, r].astype(F32) - mean[at]) * rstd[at]
            inner = grad[img, r] * gain[...] - first[at] - centred * second[at]
            out[img, r] = (u[img, r].astype(F32) + rstd[at] * inner).astype(BF16)


def body(inputs, norm_gain, norm_bias, conv_weight, upstream):
    images, rows, columns, channels = inputs.shape
    count, dps = lax.axis_size("space"), lax.axis_size("dp")
    me, half = lax.axis_index("space"), lax.axis_index("dp")
    core, mate = me & 1, me ^ 1
    groups = channels // GSIZE
    bits = count.bit_length() - 1
    size = float(rows * columns * GSIZE * count)
    block = images * columns
    two = dps == 2
    gain_row, bias_row = norm_gain[None], norm_bias[None]
    taps = conv_weight.shape[0]
    own_ok = jnp.where((me == 0) | (me == count - 1), 0, 1)
    mate_ok = jnp.where((mate == 0) | (mate == count - 1), 0, 1)
    info = jnp.stack(
        [core, own_ok, mate_ok, half if two else 0 * core, me]
    ).astype(jnp.int32)

    pairs = []
    for i in range(1, count - 1, 2):
        pairs += [(i, i + 1), (i + 1, i)]
    x_mate = swap(inputs, "space", 1)
    u_mate = swap(upstream, "space", 1)

    part = conv_weight.shape[1] // 2
    row_shape = (images, columns, channels)
    first_info = info
    if two:
        w_sent = kernel_call(
            slice_kernel, 8, struct((taps, part, channels), BF16), [S, H], "slice",
            [pltpu.SemaphoreType.DMA],
        )(info, in_hbm(conv_weight))
        w_low = swap(w_sent, "dp", 1)
        first_info = after(info, w_sent)
    stats, edge_x, edge_u = kernel_call(
        stats_kernel, 16,
        (struct((2 * images, groups), F32), struct(row_shape, BF16), struct(row_shape, BF16)),
        [S, V, H], "stats", [pltpu.SemaphoreType.DMA((2,))],
    )(first_info, inputs, in_hbm(upstream))
    rim_x = lax.ppermute(edge_x, "space", pairs)
    lhs = kernel_call(
        functools.partial(turn_kernel, bits), 16, struct((channels // 2, 4 * block), BF16),
        [S, V, V], "turn", [pltpu.VMEM((4 * block, channels), BF16)],
    )(info, upstream, u_mate)
    for place in [0] + list(range(2, bits)) + [1]:
        if place == 1:
            stats, rim_x = lax.optimization_barrier((stats, rim_x))
        step = swap(stats, "space", 1 << place)
        if place == 2:
            step, lhs = lax.optimization_barrier((step, lhs))
        stats = stats + step
    rim_x_mate = swap(rim_x, "space", 1)
    rim_u = lax.ppermute(after(edge_u, stats), "space", pairs)

    act_mid, act_side, mean, rstd = kernel_call(
        functools.partial(act_kernel, size), 24,
        (
            struct((6 * block, channels), BF16),
            struct((2, 6 * block, channels), BF16),
            struct((images, channels), F32),
            struct((images, channels), F32),
        ),
        [S] + [V] * 7, "activate",
    )(info, stats, inputs, x_mate, rim_x, rim_x_mate, gain_row, bias_row)

    def fold(kept, got):
        shape = (kept.shape[0] // 2, kept.shape[1])
        return kernel_call(
            fold_kernel, 8, (struct(shape, BF16), struct(shape, F32)), [V, V], "fold"
        )(kept, got)

    def split(kept, got):
        shape = (kept.shape[0], kept.shape[1] // 2)
        return kernel_call(
            functools.partial(part_kernel, channels // 2), 8,
            (struct(shape, BF16), struct(shape, F32)), [S, V, V], "split",
        )(info, kept, got)

    width_a, width_b = len(GROUP_A) * channels, len(GROUP_B) * channels
    shape_b = (channels // 2, width_b // 2) if two else (channels // 4, width_b)
    shapes = [((channels // 4, width_a), BF16), ((channels // 4, width_a), F32)]
    shapes += [(shape_b, BF16), (shape_b, F32)]
    sent_a, kept_a, sent_b, kept_b = kernel_call(
        functools.partial(grad_kernel, block, two), 28,
        tuple(pltpu.HBM(*shape) for shape in shapes), [S] + [V] * 3, "weight_terms",
        [pltpu.VMEM(*shape) for shape in shapes] + [pltpu.SemaphoreType.DMA((10,))], (H,) * 4,
    )(info, lhs, act_mid, act_side)
    sent_a, sent_b, rim_u = lax.optimization_barrier((sent_a, sent_b, rim_u))
    got_a = swap(sent_a, "space", 4)
    got_b = swap(sent_b, "dp", 1) if two else swap(sent_b, "space", 4)

    if two:
        w_low = after(w_low, sent_b)
        other = (1 - half) * 2 * part
        spots = jnp.stack([half * 2 * part, other + core * part, other + (1 - core) * part])
        w_parts = [conv_weight, w_low, swap(w_low, "space", 1)]
    else:
        spots = jnp.zeros((1,), jnp.int32)
        w_parts = [lax.all_gather(conv_weight, "dp", axis=1, tiled=True)]
    grad, sums, weights = kernel_call(
        back_kernel, 32,
        (
            struct(inputs.shape, F32),
            struct((40, LANES), F32),
            struct((taps, channels, channels), BF16),
        ),
        [S, S] + [H] * len(w_parts) + [V, V, H] + [V] * 5, "conv_backward",
        [
            pltpu.VMEM((3, 4 * block, channels), BF16),
            pltpu.VMEM(row_shape, BF16),
            pltpu.VMEM((images, channels), F32),
            pltpu.VMEM((images, channels), F32),
            pltpu.SemaphoreType.DMA((taps, len(w_parts))),
            pltpu.SemaphoreType.DMA,
        ],
    )(
        after(info, sent_b), spots.astype(jnp.int32), *[in_hbm(value) for value in w_parts],
        upstream, u_mate, in_hbm(rim_u), inputs, mean, rstd, gain_row, bias_row,
    )

    base = images + images % 2
    last = base + 2 * channels // LANES
    for place in range(2):
        sums = sums + swap(sums, "space", 1 << place)
    if two:
        sent_a, kept_a = split(kept_a, after(got_a, sums))
        got_a = swap(sent_a, "dp", 1)
        sent_b, kept_b = fold(kept_b, after(got_b, sent_a))
        got_b = swap(sent_b, "space", 2)
    own = kernel_call(
        functools.partial(own_kernel, columns), 16, struct((3, 4 * block, channels), BF16),
        [S, V], "own",
    )(after(info, sent_b), act_mid)
    for place in range(2, bits):
        step = swap(sums, "space", 1 << place)
        if place == 2:
            step, own = lax.optimization_barrier((step, own))
        if place == 3:
            first_row = kernel_call(
                conv_first_kernel, 32, struct(row_shape, BF16), [V] * 3, "conv_forward"
            )(after(own, sums), weights, inputs)
            step, first_row = lax.optimization_barrier((step, first_row))
        sums = sums + step
    sent_a, kept_a = fold(kept_a, after(got_a, sums))
    got_a = swap(sent_a, "space", 2)
    sent_b, kept_b = fold(kept_b, after(got_b, sent_a))
    got_b = swap(sent_b, "space", 4 if two else 2)
    sums = after(sums, sent_b)
    input_grad = kernel_call(
        functools.partial(input_kernel, size), 16, struct(inputs.shape, BF16), [V] * 7, "input_grad"
    )(sums, grad, inputs, upstream, mean, rstd, gain_row)
    totals = sums[base:last]
    more = swap(totals, "dp", 1) if two else lax.psum(totals, "dp")
    sent_a, kept_a = fold(kept_a, after(got_a, input_grad))
    got_a = swap(sent_a, "space", 8)
    sent_b, kept_b = fold(kept_b, after(got_b, sent_a))
    got_b = swap(sent_b, "space", 8)
    mixed = kernel_call(
        conv_kernel, 32, struct(inputs.shape, BF16), [V] * 4, "conv_forward"
    )(after(own, sent_b), weights, inputs, first_row)
    got_a, more = lax.optimization_barrier((got_a, more, mixed))[:2]
    totals = (totals + more if two else more).reshape(2, channels)
    wide = channels // 2 if two else channels
    weight_grad = kernel_call(
        last_kernel, 16, struct((taps, kept_a.shape[0], wide), F32), [V] * 4, "last"
    )(kept_a, got_a, kept_b, got_b)
    if not two:
        weight_grad = lax.psum_scatter(weight_grad, "dp", scatter_dimension=2, tiled=True)
    weight_grad = weight_grad.transpose(0, 2, 1)
    return (mixed, input_grad, weight_grad, totals[0], totals[1])


def solution(mesh):
    in_specs = (
        P("dp", "space", None, None),
        P(),
        P(),
        P(None, "dp", None),
        P("dp", "space", None, None),
    )
    out_specs = (
        P("dp", "space", None, None),
        P("dp", "space", None, None),
        P(None, "dp", "space"),
        P(),
        P(),
    )
    return jax.shard_map(body, mesh=mesh, in_specs=in_specs, out_specs=out_specs, check_vma=False)
```

```python
import functools

import jax
import jax.numpy as jnp
from jax import lax
from jax.experimental import pallas as pl
from jax.experimental.pallas import tpu as pltpu
from jax.sharding import PartitionSpec as P

GSIZE = 40
EPS = 1e-05
GROUP_A, GROUP_B = (0, 1, 2, 3), (4, 5, 6, 7, 8)
LANES = 128
F32 = jnp.float32
BF16 = jnp.bfloat16
HIGHEST = lax.Precision.HIGHEST
VMEM_SPEC = pl.BlockSpec(memory_space=pltpu.VMEM)
SMEM_SPEC = pl.BlockSpec(memory_space=pltpu.SMEM)
HBM_SPEC = pl.BlockSpec(memory_space=pltpu.HBM)
MIB = 1 << 20
V, S, H = VMEM_SPEC, SMEM_SPEC, HBM_SPEC


def kernel_call(body, mib, out_shape, in_specs, name, scratch=(), out_specs=None):
    return pl.pallas_call(
        body,
        out_shape=out_shape,
        in_specs=in_specs,
        out_specs=out_specs or jax.tree.map(lambda _: VMEM_SPEC, out_shape),
        scratch_shapes=scratch,
        compiler_params=pltpu.CompilerParams(vmem_limit_bytes=mib * MIB),
        name=name,
    )


def struct(shape, dtype):
    return jax.ShapeDtypeStruct(shape, dtype)


def swap(value, axis, bit):
    count = lax.axis_size(axis)
    return lax.ppermute(value, axis, [(i, i ^ bit) for i in range(count)])


def in_hbm(value):
    return pltpu.with_memory_space_constraint(value, pltpu.HBM)


def after(value, *others):
    return lax.optimization_barrier((value,) + others)[0]


def members(channels, groups):
    chan = lax.broadcasted_iota(jnp.int32, (groups, channels), 1)
    first = lax.broadcasted_iota(jnp.int32, (groups, channels), 0) * GSIZE
    return ((chan >= first) & (chan < first + GSIZE)).astype(F32)


def to_groups(sums, member):
    return lax.dot_general(
        sums, member, (((1,), (1,)), ((), ())), precision=HIGHEST, preferred_element_type=F32
    )


def to_chans(values, member):
    return jnp.dot(values, member, precision=HIGHEST, preferred_element_type=F32)


def shifted(block):
    columns = block.shape[0]
    col = lax.broadcasted_iota(jnp.int32, block.shape, 0)
    down = jnp.where(col == 0, 0.0, pltpu.roll(block, 1, axis=0))
    up = jnp.where(col == columns - 1, 0.0, pltpu.roll(block, columns - 1, axis=0))
    return down, up


def slice_kernel(info, w, out, sem):
    rows = out.shape[1]
    at = pl.ds(pl.multiple_of(info[0] * rows, 32), rows)
    copy = pltpu.make_async_copy(w.at[:, at, :], out, sem)
    copy.start()
    copy.wait()


def stats_kernel(info, x, u, out, edge_x, edge_u, sem):
    images, _, _, channels = x.shape
    core = info[0]
    copies = [
        pltpu.make_async_copy(x.at[:, core], edge_x, sem.at[0]),
        pltpu.make_async_copy(u.at[:, core], edge_u, sem.at[1]),
    ]
    for c in copies:
        c.start()
    one, two = [], []
    for img in range(images):
        value = x[img].astype(F32).reshape(-1, channels)
        one.append(jnp.sum(value, axis=0, keepdims=True))
        two.append(jnp.sum(value * value, axis=0, keepdims=True))
    out[...] = to_groups(jnp.concatenate(one + two), members(channels, channels // GSIZE))
    for c in copies:
        c.wait()


def act_kernel(size, info, stats, x, x_mate, rim, rim_mate, gain, bias, mid, side, mean, rstd):
    images, _, columns, channels = x.shape
    core, own_ok, mate_ok = info[0], info[1], info[2]
    member = members(channels, channels // GSIZE)
    group_mean = stats[:images] / size
    group_rstd = lax.rsqrt(stats[images:] / size - group_mean * group_mean + EPS)
    mean[...] = to_chans(group_mean, member)
    rstd[...] = to_chans(group_rstd, member)

    def fill(load, row, keep):
        def step(img, carry):
            value = load(img).astype(F32)
            scale = rstd[pl.ds(img, 1), :] * gain[...]
            normed = (value - mean[pl.ds(img, 1), :]) * scale + bias[...]
            turned = 0.5 * normed
            act = turned + turned * jnp.tanh(turned)
            if keep is not None:
                act = jnp.where(keep > 0, act, 0.0)
            down, up = shifted(act)
            at = pl.ds(pl.multiple_of((row * images + img) * columns, columns), columns)
            mid[at, :] = act.astype(BF16)
            side[0, at, :] = down.astype(BF16)
            side[1, at, :] = up.astype(BF16)
            return carry

        lax.fori_loop(0, images, step, 0)

    fill(lambda img: x[img, 0], 1 + 2 * core, None)
    fill(lambda img: x[img, 1], 2 + 2 * core, None)
    fill(lambda img: x_mate[img, 0], 3 - 2 * core, None)
    fill(lambda img: x_mate[img, 1], 4 - 2 * core, None)
    fill(lambda img: rim[img], 5 * core, own_ok)
    fill(lambda img: rim_mate[img], 5 - 5 * core, mate_ok)


def turn_kernel(bits, info, u, u_mate, out, rows):
    images, _, columns, channels = u.shape
    core, me = info[0], info[4]
    block = images * columns
    for r in range(2):
        at = pl.multiple_of((r + 2 * core) * block, 64)
        rows[pl.ds(at, block), :] = u[:, r].reshape(block, channels)
        at = pl.multiple_of((r + 2 - 2 * core) * block, 64)
        rows[pl.ds(at, block), :] = u_mate[:, r].reshape(block, channels)
    width = channels >> bits
    row = lax.broadcasted_iota(jnp.int32, out.shape[:1] + (channels,), 0)
    chan = core * width + row
    for place in range(bits - 1):
        low = width << (bits - 2 - place)
        own = (me >> (place + 1)) & 1
        late = lax.rem(row, 2 * low) >= low
        chan = chan - jnp.where(late, low, 0)
        bit = jnp.where(late, own, 1 - own)
        chan = chan + bit * (width << (place + 1))
    index = lax.broadcasted_iota(jnp.int32, chan.shape, 1)
    table = (index == chan).astype(F32).astype(BF16)
    out[...] = lax.dot_general(
        table, rows[...], (((1,), (1,)), ((), ())), preferred_element_type=F32
    ).astype(BF16)


def tap_block(mid, side, t, start, rows):
    at = pl.ds(start, rows)
    return mid[at, :] if t % 3 == 1 else side[(t % 3) // 2, at, :]


def halves(value, part):
    taps = value.shape[1] // (2 * part)
    low = [value[:, 2 * t * part : (2 * t + 1) * part] for t in range(taps)]
    high = [value[:, (2 * t + 1) * part : (2 * t + 2) * part] for t in range(taps)]
    return jnp.concatenate(low, axis=1), jnp.concatenate(high, axis=1)


def second_bit(value):
    quarter = value.shape[0] // 4
    one, two, three, four = [value[k * quarter : (k + 1) * quarter] for k in range(4)]
    return jnp.concatenate([one, three]), jnp.concatenate([two, four])


def grad_kernel(block, by_dp, info, lhs, mid, side, *refs):
    outs, stages, sem = refs[:4], refs[4:8], refs[8]
    channels = mid.shape[1]
    copies = []
    for group, cut, base in ((GROUP_A, False, 0), (GROUP_B, by_dp, 2)):
        for first in range(0, len(group), 2):
            pair = group[first : first + 2]
            rhs = [tap_block(mid, side, t, (t // 3) * block, lhs.shape[1]) for t in pair]
            rhs = rhs[0] if len(rhs) == 1 else jnp.concatenate(rhs, axis=1)
            got = jnp.dot(lhs[...], rhs, preferred_element_type=F32)
            if cut:
                low, high = halves(got, channels // 2)
                sent = jnp.where(info[3] == 0, high, low)
                kept = jnp.where(info[3] == 0, low, high)
                start = first * channels // 2
            else:
                sent, kept = second_bit(got)
                start = first * channels
            at = slice(start, start + sent.shape[1])
            stages[base][:, at] = sent.astype(BF16)
            stages[base + 1][:, at] = kept
            for k in (base, base + 1):
                copy = pltpu.make_async_copy(
                    stages[k].at[:, at], outs[k].at[:, at], sem.at[len(copies)]
                )
                copy.start()
                copies.append(copy)
    for copy in copies:
        copy.wait()


def fold_kernel(kept, got, sent_out, kept_out):
    cut = sent_out.shape[0]
    sent_out[...] = (kept[:cut] + got[:cut].astype(F32)).astype(BF16)
    kept_out[...] = kept[cut:] + got[cut:].astype(F32)


def part_kernel(part, info, kept, got, sent_out, kept_out):
    low, high = halves(kept[...] + got[...].astype(F32), part)
    sent_out[...] = jnp.where(info[3] == 0, high, low).astype(BF16)
    kept_out[...] = jnp.where(info[3] == 0, low, high)


def last_kernel(kept_a, got_a, kept_b, got_b, out):
    part = out.shape[2]
    first = 0
    for kept, got in ((kept_a, got_a), (kept_b, got_b)):
        value = kept[...] + got[...].astype(F32)
        count = value.shape[1] // part
        for t in range(count):
            out[first + t] = value[:, t * part : (t + 1) * part]
        first += count


def own_kernel(columns, info, mid, out):
    def fill(k, carry):
        at = pl.ds(pl.multiple_of(k * columns, columns), columns)
        first = pl.multiple_of(2 * info[0] * (out.shape[1] // 4), 64)
        value = mid[pl.ds(first + pl.multiple_of(k * columns, columns), columns), :]
        down, up = shifted(value.astype(F32))
        out[0, at, :] = down.astype(BF16)
        out[1, at, :] = value
        out[2, at, :] = up.astype(BF16)
        return carry

    lax.fori_loop(0, out.shape[1] // columns, fill, 0)


def conv_row(row, own, w, x):
    images, _, columns, channels = x.shape
    block = images * columns
    taps = w.shape[0]
    lhs = jnp.concatenate([
        own[t % 3, (row + t // 3) * block : (row + t // 3 + 1) * block, :] for t in range(taps)
    ], axis=1)
    value = jnp.dot(lhs, w[...].reshape(taps * channels, channels), preferred_element_type=F32)
    return (x[:, row].astype(F32) + value.reshape(images, columns, channels)).astype(BF16)


def conv_first_kernel(own, w, x, out):
    out[...] = conv_row(0, own, w, x)


def conv_kernel(own, w, x, first, out):
    out[:, 0] = first[...]
    out[:, 1] = conv_row(1, own, w, x)


def back_kernel(info, places, *refs):
    pieces, refs = refs[:-17], refs[-17:]
    u, u_mate, rim_there, x, mean, rstd, gain, bias, out, sums, w = refs[:11]
    part, rim, one, two, sem, rim_sem = refs[11:]
    images, _, columns, channels = x.shape
    block = images * columns
    taps = w.shape[0]
    core = info[0]
    copies = [
        [
            pltpu.make_async_copy(
                piece.at[t],
                w.at[t, pl.ds(pl.multiple_of(places[k], 32), piece.shape[1]), :],
                sem.at[t, k],
            )
            for k, piece in enumerate(pieces)
        ]
        for t in range(taps)
    ]
    rim_copy = pltpu.make_async_copy(rim_there, rim, rim_sem)
    rim_copy.start()
    for tap in copies[:4]:
        for c in tap:
            c.start()

    def fill(load, row):
        def step(img, carry):
            value = load(img)
            down, up = shifted(value.astype(F32))
            at = pl.ds(pl.multiple_of((row * images + img) * columns, columns), columns)
            part[0, at, :] = down.astype(BF16)
            part[1, at, :] = value
            part[2, at, :] = up.astype(BF16)
            return carry

        lax.fori_loop(0, images, step, 0)

    fill(lambda img: u[img, 0], 1)
    fill(lambda img: u[img, 1], 2)
    fill(lambda img: u_mate[img, core], 3 - 3 * core)
    rim_copy.wait()
    for tap in copies[4:]:
        for c in tap:
            c.start()
    fill(lambda img: rim[img], 3 * core)

    for group in (range(0, 4), range(4, taps)):
        for t in group:
            for c in copies[t]:
                c.wait()
        rhs = jnp.concatenate([w[t] for t in group], axis=1)
        for r in range(2):
            lhs = jnp.concatenate([
                part[2 - t % 3, (r + 2 - t // 3) * block : (r + 3 - t // 3) * block, :]
                for t in group
            ], axis=1)
            value = lax.dot_general(
                lhs, rhs, (((1,), (1,)), ((), ())), preferred_element_type=F32
            ).reshape(images, columns, channels)
            if group[0] == 0:
                out[:, r] = value
            else:
                out[:, r] += value

    def finish(img, carry):
        first = jnp.zeros((1, channels), F32)
        second = jnp.zeros((1, channels), F32)
        for r in range(2):
            centred = (x[img, r].astype(F32) - mean[pl.ds(img, 1), :]) * rstd[pl.ds(img, 1), :]
            normed = centred * gain[...] + bias[...]
            s = 0.5 + 0.5 * jnp.tanh(0.5 * normed)
            grad = out[img, r] * s * (1.0 + normed * (1.0 - s))
            out[img, r] = grad
            first = first + jnp.sum(grad, axis=0, keepdims=True)
            second = second + jnp.sum(grad * centred, axis=0, keepdims=True)
        one[pl.ds(img, 1), :] = first
        two[pl.ds(img, 1), :] = second
        return carry

    lax.fori_loop(0, images, finish, 0)
    groups = channels // GSIZE
    member = members(channels, groups)
    sums[...] = jnp.zeros_like(sums)
    sums[0:images, 0:groups] = to_groups(one[...] * gain[...], member)
    sums[0:images, groups : 2 * groups] = to_groups(two[...] * gain[...], member)
    base = images + images % 2
    rows = channels // LANES
    gain_part = jnp.sum(two[...], axis=0, keepdims=True)
    bias_part = jnp.sum(one[...], axis=0, keepdims=True)
    for k in range(rows):
        at = slice(k * LANES, (k + 1) * LANES)
        sums[base + k : base + k + 1, :] = gain_part[:, at]
        sums[base + rows + k : base + rows + k + 1, :] = bias_part[:, at]


def input_kernel(size, sums, grad, x, u, mean, rstd, gain, out):
    images, rows, columns, channels = x.shape
    groups = channels // GSIZE
    member = members(channels, groups)
    means = sums[...] / size
    first = to_chans(means[:images, :groups], member)
    second = to_chans(means[:images, groups : 2 * groups], member)
    for img in range(images):
        at = slice(img, img + 1)
        for r in range(rows):
            centred = (x[img, r].astype(F32) - mean[at]) * rstd[at]
            inner = grad[img, r] * gain[...] - first[at] - centred * second[at]
            out[img, r] = (u[img, r].astype(F32) + rstd[at] * inner).astype(BF16)


def body(inputs, norm_gain, norm_bias, conv_weight, upstream):
    images, rows, columns, channels = inputs.shape
    count, dps = lax.axis_size("space"), lax.axis_size("dp")
    me, half = lax.axis_index("space"), lax.axis_index("dp")
    core, mate = me & 1, me ^ 1
    groups = channels // GSIZE
    bits = count.bit_length() - 1
    size = float(rows * columns * GSIZE * count)
    block = images * columns
    two = dps == 2
    gain_row, bias_row = norm_gain[None], norm_bias[None]
    taps = conv_weight.shape[0]
    own_ok = jnp.where((me == 0) | (me == count - 1), 0, 1)
    mate_ok = jnp.where((mate == 0) | (mate == count - 1), 0, 1)
    info = jnp.stack(
        [core, own_ok, mate_ok, half if two else 0 * core, me]
    ).astype(jnp.int32)

    pairs = []
    for i in range(1, count - 1, 2):
        pairs += [(i, i + 1), (i + 1, i)]
    x_mate = swap(inputs, "space", 1)
    u_mate = swap(upstream, "space", 1)

    part = conv_weight.shape[1] // 2
    row_shape = (images, columns, channels)
    first_info = info
    if two:
        w_sent = kernel_call(
            slice_kernel, 8, struct((taps, part, channels), BF16), [S, H], "slice",
            [pltpu.SemaphoreType.DMA],
        )(info, in_hbm(conv_weight))
        w_low = swap(w_sent, "dp", 1)
        first_info = after(info, w_sent)
    stats, edge_x, edge_u = kernel_call(
        stats_kernel, 16,
        (struct((2 * images, groups), F32), struct(row_shape, BF16), struct(row_shape, BF16)),
        [S, V, H], "stats", [pltpu.SemaphoreType.DMA((2,))],
    )(first_info, inputs, in_hbm(upstream))
    rim_x = lax.ppermute(edge_x, "space", pairs)
    lhs = kernel_call(
        functools.partial(turn_kernel, bits), 16, struct((channels // 2, 4 * block), BF16),
        [S, V, V], "turn", [pltpu.VMEM((4 * block, channels), BF16)],
    )(info, upstream, u_mate)
    for place in [0] + list(range(2, bits)) + [1]:
        if place == 1:
            stats, rim_x = lax.optimization_barrier((stats, rim_x))
        step = swap(stats, "space", 1 << place)
        if place == 2:
            step, lhs = lax.optimization_barrier((step, lhs))
        stats = stats + step
    rim_x_mate = swap(rim_x, "space", 1)
    rim_u = lax.ppermute(after(edge_u, stats), "space", pairs)

    act_mid, act_side, mean, rstd = kernel_call(
        functools.partial(act_kernel, size), 24,
        (
            struct((6 * block, channels), BF16),
            struct((2, 6 * block, channels), BF16),
            struct((images, channels), F32),
            struct((images, channels), F32),
        ),
        [S] + [V] * 7, "activate",
    )(info, stats, inputs, x_mate, rim_x, rim_x_mate, gain_row, bias_row)

    def fold(kept, got):
        shape = (kept.shape[0] // 2, kept.shape[1])
        return kernel_call(
            fold_kernel, 8, (struct(shape, BF16), struct(shape, F32)), [V, V], "fold"
        )(kept, got)

    def split(kept, got):
        shape = (kept.shape[0], kept.shape[1] // 2)
        return kernel_call(
            functools.partial(part_kernel, channels // 2), 8,
            (struct(shape, BF16), struct(shape, F32)), [S, V, V], "split",
        )(info, kept, got)

    width_a, width_b = len(GROUP_A) * channels, len(GROUP_B) * channels
    shape_b = (channels // 2, width_b // 2) if two else (channels // 4, width_b)
    shapes = [((channels // 4, width_a), BF16), ((channels // 4, width_a), F32)]
    shapes += [(shape_b, BF16), (shape_b, F32)]
    sent_a, kept_a, sent_b, kept_b = kernel_call(
        functools.partial(grad_kernel, block, two), 28,
        tuple(pltpu.HBM(*shape) for shape in shapes), [S] + [V] * 3, "weight_terms",
        [pltpu.VMEM(*shape) for shape in shapes] + [pltpu.SemaphoreType.DMA((10,))], (H,) * 4,
    )(info, lhs, act_mid, act_side)
    sent_a, sent_b, rim_u = lax.optimization_barrier((sent_a, sent_b, rim_u))
    got_a = swap(sent_a, "space", 4)
    got_b = swap(sent_b, "dp", 1) if two else swap(sent_b, "space", 4)

    if two:
        w_low = after(w_low, sent_b)
        other = (1 - half) * 2 * part
        spots = jnp.stack([half * 2 * part, other + core * part, other + (1 - core) * part])
        w_parts = [conv_weight, w_low, swap(w_low, "space", 1)]
    else:
        spots = jnp.zeros((1,), jnp.int32)
        w_parts = [lax.all_gather(conv_weight, "dp", axis=1, tiled=True)]
    grad, sums, weights = kernel_call(
        back_kernel, 32,
        (
            struct(inputs.shape, F32),
            struct((40, LANES), F32),
            struct((taps, channels, channels), BF16),
        ),
        [S, S] + [H] * len(w_parts) + [V, V, H] + [V] * 5, "conv_backward",
        [
            pltpu.VMEM((3, 4 * block, channels), BF16),
            pltpu.VMEM(row_shape, BF16),
            pltpu.VMEM((images, channels), F32),
            pltpu.VMEM((images, channels), F32),
            pltpu.SemaphoreType.DMA((taps, len(w_parts))),
            pltpu.SemaphoreType.DMA,
        ],
    )(
        after(info, sent_b), spots.astype(jnp.int32), *[in_hbm(value) for value in w_parts],
        upstream, u_mate, in_hbm(rim_u), inputs, mean, rstd, gain_row, bias_row,
    )

    base = images + images % 2
    last = base + 2 * channels // LANES
    for place in range(2):
        sums = sums + swap(sums, "space", 1 << place)
    if two:
        sent_a, kept_a = split(kept_a, after(got_a, sums))
        got_a = swap(sent_a, "dp", 1)
        sent_b, kept_b = fold(kept_b, after(got_b, sent_a))
        got_b = swap(sent_b, "space", 2)
    own = kernel_call(
        functools.partial(own_kernel, columns), 16, struct((3, 4 * block, channels), BF16),
        [S, V], "own",
    )(after(info, sent_b), act_mid)
    for place in range(2, bits):
        step = swap(sums, "space", 1 << place)
        if place == 2:
            step, own = lax.optimization_barrier((step, own))
        if place == 3:
            first_row = kernel_call(
                conv_first_kernel, 32, struct(row_shape, BF16), [V] * 3, "conv_forward"
            )(after(own, sums), weights, inputs)
            step, first_row = lax.optimization_barrier((step, first_row))
        sums = sums + step
    sent_a, kept_a = fold(kept_a, after(got_a, sums))
    got_a = swap(sent_a, "space", 2)
    sent_b, kept_b = fold(kept_b, after(got_b, sent_a))
    got_b = swap(sent_b, "space", 4 if two else 2)
    sums = after(sums, sent_b)
    input_grad = kernel_call(
        functools.partial(input_kernel, size), 16, struct(inputs.shape, BF16), [V] * 7, "input_grad"
    )(sums, grad, inputs, upstream, mean, rstd, gain_row)
    totals = sums[base:last]
    more = swap(totals, "dp", 1) if two else lax.psum(totals, "dp")
    sent_a, kept_a = fold(kept_a, after(got_a, input_grad))
    got_a = swap(sent_a, "space", 8)
    sent_b, kept_b = fold(kept_b, after(got_b, sent_a))
    got_b = swap(sent_b, "space", 8)
    mixed = kernel_call(
        conv_kernel, 32, struct(inputs.shape, BF16), [V] * 4, "conv_forward"
    )(after(own, sent_b), weights, inputs, first_row)
    got_a, more = lax.optimization_barrier((got_a, more, mixed))[:2]
    totals = (totals + more if two else more).reshape(2, channels)
    wide = channels // 2 if two else channels
    weight_grad = kernel_call(
        last_kernel, 16, struct((taps, kept_a.shape[0], wide), F32), [V] * 4, "last"
    )(kept_a, got_a, kept_b, got_b)
    if not two:
        weight_grad = lax.psum_scatter(weight_grad, "dp", scatter_dimension=2, tiled=True)
    weight_grad = weight_grad.transpose(0, 2, 1)
    return (mixed, input_grad, weight_grad, totals[0], totals[1])


def solution(mesh):
    in_specs = (
        P("dp", "space", None, None),
        P(),
        P(),
        P(None, "dp", None),
        P("dp", "space", None, None),
    )
    out_specs = (
        P("dp", "space", None, None),
        P("dp", "space", None, None),
        P(None, "dp", "space"),
        P(),
        P(),
    )
    return jax.shard_map(body, mesh=mesh, in_specs=in_specs, out_specs=out_specs, check_vma=False)
```
